256 devices in a mesh: dp: 2 (over y_hi), expert: 16 (over y_lo, x, core), tensor: 8 (over z).
Axes of the slice: x: 4, y: 4 (y_hi: 2, y_lo: 2; y = y_hi * 2 + y_lo), z: 8, core: 2. Of those that a mesh axis runs over, the one named last changes fastest.
Arguments:
- tokens: bfloat16 [4096, 3584], P(('dp', 'expert')), may hold values from -6 to 6
- cotangent: bfloat16 [4096, 3584], P(('dp', 'expert')), may hold values from -6 to 6
- dense_gate: bfloat16 [3584, 2432], P(('dp', 'expert'), 'tensor'), may hold values from -0.09375 to 0.09375
- dense_up: bfloat16 [3584, 2432], P(('dp', 'expert'), 'tensor'), may hold values from -0.09375 to 0.09375
- dense_down: bfloat16 [2432, 3584], P('tensor', ('dp', 'expert')), may hold values from -0.125 to 0.125
- expert_gate: bfloat16 [16, 3584, 2432], P('expert', 'dp', 'tensor'), may hold values from -0.09375 to 0.09375
- expert_up: bfloat16 [16, 3584, 2432], P('expert', 'dp', 'tensor'), may hold values from -0.09375 to 0.09375
- expert_down: bfloat16 [16, 2432, 3584], P('expert', 'tensor', 'dp'), may hold values from -0.125 to 0.125
- expert_ids: int32 [4096, 2], P(('dp', 'expert')), may hold values from 0 to 15, all different within a row; in each aligned block of 128 rows (0 to 127, 128 to 255, ...) at most 24 rows name the same one
- route_weights: float32 [4096, 2], P(('dp', 'expert')), may hold values from 0.1 to 1
Outputs:
- output: bfloat16 [4096, 3584], P(('dp', 'expert'))
- input_grad: bfloat16 [4096, 3584], P(('dp', 'expert'))
- dense_gate_grad: bfloat16 [3584, 2432], P(('dp', 'expert'), 'tensor')
- dense_up_grad: bfloat16 [3584, 2432], P(('dp', 'expert'), 'tensor')
- dense_down_grad: bfloat16 [2432, 3584], P('tensor', ('dp', 'expert'))
- expert_gate_grad: bfloat16 [16, 3584, 2432], P('expert', 'dp', 'tensor')
- expert_up_grad: bfloat16 [16, 3584, 2432], P('expert', 'dp', 'tensor')
- expert_down_grad: bfloat16 [16, 2432, 3584], P('expert', 'tensor', 'dp')
The draws below stay inside these ranges and needn't reach their ends.
Inputs may be any that keep to these rules, and one draw needn't show every extreme that they name: `expert_ids`: the two experts of a token differ; among the 128 rows of one device no expert is named more than 24 times, and on some devices some expert is named exactly 24 times.
All inputs are finite; a program needn't handle non-finite values.
Results may differ from the reference program's by a relative error of at most 0.033.
Values may be sent and summed in bfloat16 or wider, within the bound.
A program may use at most 128 MiB of HBM per device.

```python
import math
import jax
import jax.numpy as jnp
import numpy as np
from jax import lax

D = 3584
DFF = 2432
EH = 2432
TOK_DEV = 128
EXPERTS = 16
CAP = 24
TOKENS = 4096
N_DP = 2
N_EXPERT = 16
N_TENSOR = 8


def shard_levels(rng, shape, cuts, low, top_value):
    factor_of = 1.0
    for dim, parts in cuts:
        heights = jax.random.uniform(jax.random.fold_in(jax.random.fold_in(rng, 6), dim), (parts,), jnp.float32, low / len(cuts), top_value / len(cuts))
        factor_of = factor_of * jnp.repeat(jnp.exp(heights), shape[dim] // parts).reshape((-1,) + (1,) * (len(shape) - 1 - dim))
    return factor_of


def routed_block(stream_key, own, number, rows, amount, top, bound, lean):
    sequence = jax.random.permutation(stream_key, amount)
    packed, ordinary = load_shares(amount, rows * top, bound, lean, True), load_shares(amount, rows * top, bound, lean, False)
    places = jnp.arange(amount)

    def named(lengths, rotation):
        used = int((lengths > 0).sum())
        fixed = max(1, used // 4)
        shifted = fixed + (places - fixed + rotation * (used - fixed)) % max(1, amount - fixed)
        return jnp.zeros((amount,), jnp.int32).at[sequence[jnp.where(places < fixed, places, shifted)]].set(jnp.asarray(lengths, jnp.int32))

    lengths = jnp.where(number % 4 == 0, named(packed, number // 4), named(ordinary, number - number // 4 - 1))
    mixed = jax.random.permutation(jax.random.fold_in(own, 3), amount)
    donor, sink = mixed[0:amount // 2 * 2:2], mixed[1:amount // 2 * 2:2]
    slack = jnp.minimum(lengths[donor] - 1, bound - lengths[sink]) // 2
    slack = jnp.where((donor == sequence[0]) | (sink == sequence[0]) | (lengths[sink] == 0), 0, jnp.maximum(slack, 0))
    shifted = jax.random.randint(jax.random.fold_in(own, 4), (amount // 2,), 0, 1 << 20) % (slack + 1)
    lengths = lengths.at[donor].add(-shifted).at[sink].add(shifted)
    members = jnp.searchsorted(jnp.cumsum(lengths), jnp.arange(rows * top), side="right").astype(jnp.int32)
    listing = members.reshape(top, rows).T
    listing = listing[jax.random.permutation(jax.random.fold_in(own, 1), rows)]
    rotation = jax.random.randint(jax.random.fold_in(own, 2), (rows, 1), 0, top)
    return jnp.take_along_axis(listing, (jnp.arange(top)[None, :] + rotation) % top, axis=1)


def load_shares(number_of, total, limit, skew, full):
    loads = [(1 << 20) // math.isqrt(rank ** skew) + 1 for rank in range(1, number_of + 1)]
    largest = limit if full else min(limit, max(-(-total // number_of), total * loads[0] // sum(loads)))
    least = 1 if total - largest >= number_of - 1 else 0
    given, surplus = [largest] + [least] * (number_of - 1), total - largest - least * (number_of - 1)
    while surplus > 0:
        candidates = [i for i in range(1, number_of) if given[i] < largest] or [i for i in range(1, number_of) if given[i] < limit]
        whole, remaining = sum([loads[i] for i in candidates]), surplus
        for i in candidates:
            extra = min(limit - given[i], max(1, remaining * loads[i] // whole), surplus)
            given[i] = given[i] + extra
            surplus = surplus - extra
    return np.array(given)


def centred(own_key, extent, width, reach, split=(), held_as=jnp.bfloat16):
    result = width * jax.random.normal(own_key, extent, jnp.float32)
    if split:
        result = result * shard_levels(own_key, extent, split, -0.22, 0.18)
    return jnp.clip(result, -reach, reach).astype(held_as)


def setup_inputs(seed: int = 0) -> dict:
    splits = jax.random.split(jax.random.key(seed), 11)
    tokens = centred(splits[0], (TOKENS, D), 1.0, 6.0, ((0, 32),))
    cotangent = centred(splits[1], (TOKENS, D), 1.0, 6.0, ((0, 32),))
    dense_gate = centred(splits[2], (D, DFF), D ** -0.5, 0.09375, ((0, 32), (1, 8)))
    dense_up = centred(splits[3], (D, DFF), D ** -0.5, 0.09375, ((0, 32), (1, 8)))
    dense_down = centred(splits[4], (DFF, D), DFF ** -0.5, 0.125, ((0, 8), (1, 32)))
    expert_gate = centred(splits[5], (EXPERTS, D, EH), D ** -0.5, 0.09375, ((0, 16), (1, 2), (2, 8)))
    expert_up = centred(splits[6], (EXPERTS, D, EH), D ** -0.5, 0.09375, ((0, 16), (1, 2), (2, 8)))
    expert_down = centred(splits[7], (EXPERTS, EH, D), EH ** -0.5, 0.125, ((0, 16), (1, 8), (2, 2)))
    expert_ids_keys = jax.random.split(jax.random.fold_in(splits[8], 1), TOKENS // TOK_DEV)
    expert_ids_turns = jax.random.permutation(jax.random.fold_in(splits[8], 3), TOKENS // TOK_DEV)
    expert_ids = jax.vmap(lambda own, number: routed_block(jax.random.fold_in(splits[8], 2), own, number, TOK_DEV, EXPERTS, 2, CAP, 2))(expert_ids_keys, expert_ids_turns).reshape((TOKENS, 2))
    route_weights = jnp.clip(jnp.exp(math.log(1.0) - 2.3025851 * jax.random.uniform(splits[9], (TOKENS, 2), jnp.float32) ** shard_levels(splits[9], (TOKENS, 2), ((0, 32),), -0.2, 0.2)), 0.1, 1.0)
    return dict(tokens=tokens, cotangent=cotangent, dense_gate=dense_gate, dense_up=dense_up, dense_down=dense_down, expert_gate=expert_gate, expert_up=expert_up, expert_down=expert_down, expert_ids=expert_ids, route_weights=route_weights)


row_block = 128


def silu_pair(values):
    logistic = jax.nn.sigmoid(values)
    return values * logistic, logistic * (1.0 + values * (1.0 - logistic))


def product(left, right):
    return jnp.dot(left, right, preferred_element_type=jnp.float32)


def times_transposed(left, right):
    return lax.dot_general(left, right, (((1,), (1,)), ((), ())), preferred_element_type=jnp.float32)


def transposed_times(left, right):
    return lax.dot_general(left, right, (((0,), (0,)), ((), ())), preferred_element_type=jnp.float32)


def rounded(values):
    return lax.optimization_barrier(values.astype(jnp.bfloat16)).astype(jnp.float32)


def reference(tokens, cotangent, dense_gate, dense_up, dense_down, expert_gate, expert_up, expert_down, expert_ids, route_weights):
    token_count, model_width = tokens.shape
    dense_width = dense_gate.shape[1]
    block_width = dense_width // N_TENSOR
    pre_gate = product(tokens, dense_gate)
    pre_up = product(tokens, dense_up)
    active, slope = silu_pair(pre_gate)
    hidden = (active * pre_up).astype(jnp.bfloat16)
    grad_hidden = times_transposed(cotangent, dense_down)
    grad_gate = (grad_hidden * pre_up * slope).astype(jnp.bfloat16)
    grad_up = (grad_hidden * active).astype(jnp.bfloat16)
    dense_out = jnp.zeros((token_count, model_width), jnp.float32)
    dense_back = jnp.zeros((token_count, model_width), jnp.float32)
    for block_index in range(N_TENSOR):
        first = block_index * block_width
        last = first + block_width
        dense_out = dense_out + rounded(product(hidden[:, first:last], dense_down[first:last]))
        dense_back = dense_back + rounded(times_transposed(grad_gate[:, first:last], dense_gate[:, first:last]) + times_transposed(grad_up[:, first:last], dense_up[:, first:last]))

    replicas = N_DP * N_EXPERT
    group_rows = token_count // replicas

    def group_step(carry, pieces):
        x_group, hidden_group, cot_group, gate_group, up_group = pieces
        return (carry[0] + rounded(transposed_times(x_group, gate_group)), carry[1] + rounded(transposed_times(x_group, up_group)), carry[2] + rounded(transposed_times(hidden_group, cot_group))), None

    pieces = tuple(v.reshape(replicas, group_rows, v.shape[1]) for v in (tokens, hidden, cotangent, grad_gate, grad_up))
    start_sums = (jnp.zeros((model_width, dense_width), jnp.float32), jnp.zeros((model_width, dense_width), jnp.float32), jnp.zeros((dense_width, model_width), jnp.float32))
    (gate_sum, up_sum, down_sum), _ = lax.scan(group_step, start_sums, pieces)

    experts = expert_gate.shape[0]
    hidden_width = expert_gate.shape[2]
    expert_block = hidden_width // N_TENSOR
    pairs = 2 * token_count
    pair_expert = expert_ids.reshape(-1).astype(jnp.int32)
    pair_token = (jnp.arange(pairs, dtype=jnp.int32) // 2).astype(jnp.int32)
    pair_replica = (pair_token // (token_count // N_DP)).astype(jnp.int32)
    pair_key = (pair_replica * experts + pair_expert).astype(jnp.int32)
    pair_gate = route_weights.reshape(-1).astype(jnp.float32)
    keys = N_DP * experts
    order = jnp.argsort(pair_key, stable=True).astype(jnp.int32)
    counts = jnp.sum((pair_key[None, :] == jnp.arange(keys, dtype=jnp.int32)[:, None]).astype(jnp.int32), axis=1).astype(jnp.int32)
    starts = (jnp.cumsum(counts) - counts).astype(jnp.int32)
    padded = jnp.concatenate([order, jnp.zeros((row_block,), jnp.int32)])

    def expert_step(carry, expert_index):
        moe_out, moe_back = carry
        weight_gate = lax.dynamic_index_in_dim(expert_gate, expert_index, 0, keepdims=False)
        weight_up = lax.dynamic_index_in_dim(expert_up, expert_index, 0, keepdims=False)
        weight_down = lax.dynamic_index_in_dim(expert_down, expert_index, 0, keepdims=False)
        sum_gate = jnp.zeros((model_width, hidden_width), jnp.float32)
        sum_up = jnp.zeros((model_width, hidden_width), jnp.float32)
        sum_down = jnp.zeros((hidden_width, model_width), jnp.float32)
        for replica in range(N_DP):
            key_index = (replica * experts + expert_index).astype(jnp.int32)
            count = counts[key_index]
            start = starts[key_index]

            def keep_going(inner):
                return inner[0] * row_block < count

            def one_block(inner):
                block_number, moe_out, moe_back, acc_gate, acc_up, acc_down = inner
                base = block_number * row_block
                chosen = lax.dynamic_slice_in_dim(padded, (start + base).astype(jnp.int32), row_block)
                valid = (jnp.arange(row_block, dtype=jnp.int32) + base) < count
                token_index = pair_token[chosen]
                weight = jnp.where(valid, pair_gate[chosen], jnp.zeros((row_block,), jnp.float32))
                rows = tokens[token_index]
                cot_rows = (cotangent[token_index].astype(jnp.float32) * weight[:, None]).astype(jnp.bfloat16)
                row_gate = product(rows, weight_gate)
                row_up = product(rows, weight_up)
                row_active, row_slope = silu_pair(row_gate)
                row_hidden = (row_active * row_up).astype(jnp.bfloat16)
                grad_act = times_transposed(cot_rows, weight_down)
                row_grad_gate = (grad_act * row_up * row_slope).astype(jnp.bfloat16)
                row_grad_up = (grad_act * row_active).astype(jnp.bfloat16)
                out_sum = jnp.zeros((row_block, model_width), jnp.float32)
                back_sum = jnp.zeros((row_block, model_width), jnp.float32)
                for part in range(N_TENSOR):
                    first = part * expert_block
                    last = first + expert_block
                    out_sum = out_sum + rounded(product(row_hidden[:, first:last], weight_down[first:last]))
                    back_sum = back_sum + rounded(times_transposed(row_grad_gate[:, first:last], weight_gate[:, first:last]) + times_transposed(row_grad_up[:, first:last], weight_up[:, first:last]))
                moe_out = moe_out.at[token_index].add(weight[:, None] * rounded(out_sum))
                back_rows = jnp.where(valid[:, None], rounded(back_sum), jnp.zeros((row_block, model_width), jnp.float32))
                moe_back = moe_back.at[token_index].add(back_rows)
                acc_gate = acc_gate + transposed_times(rows, row_grad_gate)
                acc_up = acc_up + transposed_times(rows, row_grad_up)
                acc_down = acc_down + transposed_times(row_hidden, cot_rows)
                return (block_number + 1, moe_out, moe_back, acc_gate, acc_up, acc_down)

            inner = (jnp.int32(0), moe_out, moe_back, jnp.zeros((model_width, hidden_width), jnp.float32), jnp.zeros((model_width, hidden_width), jnp.float32), jnp.zeros((hidden_width, model_width), jnp.float32))
            _, moe_out, moe_back, acc_gate, acc_up, acc_down = lax.while_loop(keep_going, one_block, inner)
            sum_gate = sum_gate + rounded(acc_gate)
            sum_up = sum_up + rounded(acc_up)
            sum_down = sum_down + rounded(acc_down)
        return (moe_out, moe_back), (sum_gate.astype(jnp.bfloat16), sum_up.astype(jnp.bfloat16), sum_down.astype(jnp.bfloat16))

    start_state = (jnp.zeros((token_count, model_width), jnp.float32), jnp.zeros((token_count, model_width), jnp.float32))
    (moe_out, moe_back), (grad_one, grad_three, grad_two) = lax.scan(expert_step, start_state, jnp.arange(experts, dtype=jnp.int32))
    output = (tokens.astype(jnp.float32) + dense_out + moe_out).astype(jnp.bfloat16)
    input_grad = (cotangent.astype(jnp.float32) + dense_back + moe_back).astype(jnp.bfloat16)
    return (output, input_grad, gate_sum.astype(jnp.bfloat16), up_sum.astype(jnp.bfloat16), down_sum.astype(jnp.bfloat16), grad_one, grad_three, grad_two)
```

```python
import functools

import jax
import jax.numpy as jnp
from jax import lax
from jax.experimental import pallas as pl
from jax.experimental.pallas import tpu as pltpu
from jax.sharding import PartitionSpec as P

MESH = pl.DeviceIdType.MESH
BF = jnp.bfloat16
F32 = jnp.float32
HBM = pl.BlockSpec(memory_space=pl.ANY)
VMEM = pl.BlockSpec(memory_space=pltpu.VMEM)
DMA = pltpu.SemaphoreType.DMA
ROWS_A = pl.ds(0, 48)
ROWS_B = pl.ds(48, 64)


def silu_pair(values):
    logistic = jax.nn.sigmoid(values)
    return (values * logistic, logistic * (1.0 + values * (1.0 - logistic)))


def product(left, right):
    return jnp.dot(left, right, preferred_element_type=F32)


def times_transposed(left, right):
    return lax.dot_general(left, right, (((1,), (1,)), ((), ())), preferred_element_type=F32)


def transposed_times(left, right):
    return lax.dot_general(left, right, (((0,), (0,)), ((), ())), preferred_element_type=F32)


def place():
    dp, e, z = lax.axis_index("dp"), lax.axis_index("expert"), lax.axis_index("tensor")
    return dp * 2 + e // 8, (e // 2) % 4, e % 2, z


def device(y, x, c, z):
    return (y // 2, (y % 2) * 8 + x * 2 + c, z)


def dispatch_dest(y, x, c, z, j):
    return (y + j) % 4, (x + z // 2 + 2 * (j % 2)) % 4, (c + z) % 2


def dispatch_source(y, x, c, z, j):
    return (y + 4 - j) % 4, (x + 8 - z // 2 - 2 * (j % 2)) % 4, (c + z) % 2


def remote(src, dst, send_sem, recv_sem, dev):
    return pltpu.make_async_remote_copy(
        src_ref=src, dst_ref=dst, send_sem=send_sem, recv_sem=recv_sem, device_id=dev, device_id_type=MESH
    )


def greet(devices, conditional=()):
    barrier = pltpu.get_barrier_semaphore()
    for dev in devices:
        pl.semaphore_signal(barrier, inc=1, device_id=dev, device_id_type=MESH)
    for cond, dev in conditional:
        @pl.when(cond)
        def _():
            pl.semaphore_signal(barrier, inc=1, device_id=dev, device_id_type=MESH)
    count = jnp.int32(len(devices))
    for cond, dev in conditional:
        count = count + jnp.where(cond, jnp.int32(1), jnp.int32(0))
    pl.semaphore_wait(barrier, count)


def gather_kernel(send, w, recv, full, dsp_s, dsp_r, ring_s, ring_r, loc, d_s, d_r):
    y, x, c, z = place()
    right, left = device(y, x, c, (z + 1) % 8), device(y, x, c, (z + 7) % 8)
    xs = [device(y, (x + i) % 4, c, z) for i in (1, 2, 3)]
    ys = [device((y + i) % 4, x, c, z) for i in (1, 2, 3)]
    other = device(y, x, 1 - c, z)
    dests = [dispatch_dest(y, x, c, z, j) for j in range(4)]
    sources = [dispatch_source(y, x, c, z, j) for j in range(4)]
    greet(
        [device(*s, z) for s in sources[1:]] + xs + ys + [other, left, right],
        [(z != 0, device(*sources[0], z))],
    )

    def disp(j):
        return remote(send.at[(y + j) % 4], recv.at[z, y], dsp_s.at[j], dsp_r.at[j], device(*dests[j], z))

    here = pltpu.make_async_copy(send.at[y], recv.at[z, y], dsp_r.at[0])

    def hop(direction, t, j):
        origin = (z + 9 - t) % 8 if direction == 0 else (z + t - 1) % 8
        k = (y + 4 - j) % 4
        return remote(
            recv.at[origin, k], recv.at[origin, k],
            ring_s.at[direction, t - 1, j], ring_r.at[direction, t - 1, j], (right, left)[direction],
        )

    def members(direction, t):
        return range(4) if t < 4 else ((0, 1), (2, 3))[direction]

    @pl.when(z == 0)
    def _():
        here.start()

    @pl.when(z != 0)
    def _():
        disp(0).start()

    for j in (1, 2, 3):
        disp(j).start()

    own = pltpu.make_async_copy(w, full.at[y, x, c], loc.at[0])
    own.start()
    one_a = [remote(w.at[ROWS_A], full.at[y, x, c, ROWS_A], d_s.at[0, i], d_r.at[0, i], xs[i]) for i in range(3)]
    one_b = [remote(w.at[ROWS_B], full.at[y, x, c, ROWS_B], d_s.at[1, i], d_r.at[1, i], ys[i]) for i in range(3)]
    two_a = [
        remote(full.at[y, :, c, ROWS_A], full.at[y, :, c, ROWS_A], d_s.at[2, i], d_r.at[2, i], ys[i]) for i in range(3)
    ]
    two_b = [
        remote(full.at[:, x, c, ROWS_B], full.at[:, x, c, ROWS_B], d_s.at[3, i], d_r.at[3, i], xs[i]) for i in range(3)
    ]
    three = [remote(full.at[i, :, c], full.at[i, :, c], d_s.at[4, i], d_r.at[4, i], other) for i in range(4)]
    for copy in one_a + one_b:
        copy.start()

    for j in range(4):
        if j == 0:
            @pl.when(z == 0)
            def _():
                here.wait()

            @pl.when(z != 0)
            def _():
                disp(0).wait_recv()
        else:
            disp(j).wait_recv()
        hop(0, 1, j).start()
        hop(1, 1, j).start()
    own.wait()
    for copy in one_a + one_b:
        copy.wait_recv()
    for copy in two_a + two_b:
        copy.start()
    for t in (2, 3, 4):
        for j in range(4):
            for direction in (0, 1):
                hop(direction, t - 1, j).wait_recv()
                if j in members(direction, t):
                    hop(direction, t, j).start()
        if t == 3:
            for copy in two_a + two_b:
                copy.wait_recv()
            for copy in three:
                copy.start()
    for direction in (0, 1):
        for j in members(direction, 4):
            hop(direction, 4, j).wait_recv()
    for copy in three:
        copy.wait_recv()

    @pl.when(z != 0)
    def _():
        disp(0).wait_send()

    for j in (1, 2, 3):
        disp(j).wait_send()
    for direction in (0, 1):
        for t in (1, 2, 3, 4):
            for j in members(direction, t):
                hop(direction, t, j).wait_send()
    for copy in one_a + one_b + two_a + two_b + three:
        copy.wait_send()


def gather_call(send, w):
    return pl.pallas_call(
        gather_kernel,
        out_shape=(
            jax.ShapeDtypeStruct((8, 4, 48, send.shape[2]), BF),
            jax.ShapeDtypeStruct((4, 4, 2) + w.shape, BF),
        ),
        in_specs=[HBM, HBM],
        out_specs=(HBM, HBM),
        scratch_shapes=[DMA((4,)), DMA((4,)), DMA((2, 4, 4)), DMA((2, 4, 4)), DMA((1,)), DMA((5, 4)), DMA((5, 4))],
        compiler_params=pltpu.CompilerParams(collective_id=0, has_side_effects=True),
    )(send, w)


def swap_kernel(mine, theirs, via, s1, r1, s2, r2):
    y, x, c, z = place()
    up, down = device((y + 1) % 4, x, c, z), device((y + 3) % 4, x, c, z)
    greet([up, down])
    near = [remote(mine.at[i], via.at[i], s1.at[i], r1.at[i], (up, down)[i % 2]) for i in range(8)]
    far = [remote(via.at[i], theirs.at[i], s2.at[i], r2.at[i], (up, down)[i % 2]) for i in range(8)]
    for copy in near:
        copy.start()
    for i in range(8):
        near[i].wait_recv()
        far[i].start()
    for copy in far:
        copy.wait_recv()
    for copy in near + far:
        copy.wait_send()


def swap_call(mine):
    shape = jax.ShapeDtypeStruct(mine.shape, BF)
    return pl.pallas_call(
        swap_kernel,
        out_shape=(shape, shape),
        in_specs=[HBM],
        out_specs=(HBM, HBM),
        scratch_shapes=[DMA((8,)), DMA((8,)), DMA((8,)), DMA((8,))],
        compiler_params=pltpu.CompilerParams(collective_id=1, has_side_effects=True),
    )(mine)[0]


def add_into(dst, *others):
    total = dst[...].astype(F32)
    for other in others:
        total = total + other[...].astype(F32)
    dst[...] = total.astype(BF)


def scatter_kernel(part, dw, ret, grad, rr, cr, ra, rb, rc, rd, ring_s, ring_r, ret_s, ret_r, d_s, d_r):
    y, x, c, z = place()
    right, left = device(y, x, c, (z + 1) % 8), device(y, x, c, (z + 7) % 8)
    xi = [(x + i) % 4 for i in (1, 2, 3)]
    yi = [(y + i) % 4 for i in (1, 2, 3)]
    xs = [device(y, i, c, z) for i in xi]
    ys = [device(i, x, c, z) for i in yi]
    other = device(y, x, 1 - c, z)
    dests = [dispatch_dest(y, x, c, z, j) for j in range(4)]
    sources = [dispatch_source(y, x, c, z, j) for j in range(4)]
    greet(
        [device(*d, z) for d in dests[1:]] + xs + ys + [other, left, right],
        [(z != 0, device(*dests[0], z))],
    )

    def target(direction, u):
        return (z + 5 - u) % 8 if direction == 0 else (z + 3 + u) % 8

    def hop(direction, u, k):
        src = part.at[target(direction, u), k] if (u == 1 or (u == 2 and k not in members(direction, 1))) else rr.at[direction, u - 2, k]
        return remote(
            src, rr.at[direction, u - 1, k],
            ring_s.at[direction, u - 1, k], ring_r.at[direction, u - 1, k], (right, left)[direction],
        )

    def members(direction, u):
        return range(4) if u > 1 else ((0, 1), (2, 3))[direction]

    for direction in (0, 1):
        for k in members(direction, 1):
            hop(direction, 1, k).start()
    one = [remote(dw.at[i, :, 1 - c], cr.at[i], d_s.at[0, i], d_r.at[0, i], other) for i in range(4)]
    for copy in one:
        copy.start()
    for direction in (0, 1):
        for k in range(4):
            if k not in members(direction, 1):
                hop(direction, 2, k).start()
    for copy in one:
        copy.wait_recv()

    @pl.loop(0, 16)
    def _(i):
        add_into(cr.at[i // 4, i % 4], dw.at[i // 4, i % 4, c])

    for copy in one:
        copy.wait_send()
    two_a = [remote(cr.at[yi[i], :, ROWS_A], ra.at[i], d_s.at[1, i], d_r.at[1, i], ys[i]) for i in range(3)]
    two_b = [remote(cr.at[:, xi[i], ROWS_B], rb.at[i], d_s.at[2, i], d_r.at[2, i], xs[i]) for i in range(3)]
    for copy in two_a + two_b:
        copy.start()

    def ring_step(u):
        for k in range(4):
            for direction in (0, 1):
                if u == 2 and k not in members(direction, 1):
                    continue
                hop(direction, u - 1, k).wait_recv()
                add_into(rr.at[direction, u - 2, k], part.at[target(direction, u), k])
                hop(direction, u, k).start()

    ring_step(2)
    for copy in two_a + two_b:
        copy.wait_recv()

    @pl.loop(0, 4)
    def _(i):
        add_into(cr.at[y, i, ROWS_A], ra.at[0, i], ra.at[1, i], ra.at[2, i])
        add_into(cr.at[i, x, ROWS_B], rb.at[0, i], rb.at[1, i], rb.at[2, i])

    three_a = [remote(cr.at[y, xi[i], ROWS_A], rc.at[i], d_s.at[3, i], d_r.at[3, i], xs[i]) for i in range(3)]
    three_b = [remote(cr.at[yi[i], x, ROWS_B], rd.at[i], d_s.at[4, i], d_r.at[4, i], ys[i]) for i in range(3)]
    for copy in three_a + three_b:
        copy.start()
    ring_step(3)
    for copy in three_a + three_b:
        copy.wait_recv()
    add_into(cr.at[y, x, ROWS_A], rc.at[0], rc.at[1], rc.at[2])
    add_into(cr.at[y, x, ROWS_B], rd.at[0], rd.at[1], rd.at[2])
    grad[...] = cr[y, x]
    ring_step(4)

    def home(j):
        return remote(
            rr.at[0, 3, (y + 4 - j) % 4], ret.at[y], ret_s.at[j], ret_r.at[j], device(*sources[j], z)
        )

    here = pltpu.make_async_copy(rr.at[0, 3, y], ret.at[y], ret_r.at[0])
    for k in range(4):
        hop(0, 4, k).wait_recv()
        hop(1, 4, k).wait_recv()
        add_into(rr.at[0, 3, k], rr.at[1, 3, k], part.at[z, k])

    @pl.when(z == 0)
    def _():
        here.start()

    @pl.when(z != 0)
    def _():
        home(0).start()

    for j in (1, 2, 3):
        home(j).start()

    @pl.when(z == 0)
    def _():
        here.wait()

    @pl.when(z != 0)
    def _():
        home(0).wait()

    for j in (1, 2, 3):
        home(j).wait()
    for direction in (0, 1):
        for u in (1, 2, 3, 4):
            for k in members(direction, u):
                hop(direction, u, k).wait_send()
    for copy in two_a + two_b + three_a + three_b:
        copy.wait_send()


def scatter_call(part, dw):
    width, lanes = part.shape[3], dw.shape[4]
    return pl.pallas_call(
        scatter_kernel,
        out_shape=(
            jax.ShapeDtypeStruct((4, 48, width), BF),
            jax.ShapeDtypeStruct((112, lanes), BF),
        ),
        in_specs=[VMEM, VMEM],
        out_specs=(HBM, VMEM),
        scratch_shapes=[
            pltpu.VMEM((2, 4, 4, 48, width), BF),
            pltpu.VMEM((4, 4, 112, lanes), BF),
            pltpu.VMEM((3, 4, 48, lanes), BF),
            pltpu.VMEM((3, 4, 64, lanes), BF),
            pltpu.VMEM((3, 48, lanes), BF),
            pltpu.VMEM((3, 64, lanes), BF),
            DMA((2, 4, 4)), DMA((2, 4, 4)), DMA((4,)), DMA((4,)), DMA((5, 4)), DMA((5, 4)),
        ],
        compiler_params=pltpu.CompilerParams(
            collective_id=2, has_side_effects=True, vmem_limit_bytes=56 * 1024 * 1024
        ),
    )(part, dw)


def finish_kernel(part, tokens, cots, out, back, rr, rs_s, rs_r, ag_s, ag_r):
    y, x, c, z = place()
    right, left = device(y, x, c, (z + 1) % 8), device(y, x, c, (z + 7) % 8)
    greet([left, right])
    outs = (out, back)

    def target(direction, u):
        return (z + 5 - u) % 8 if direction == 0 else (z + 3 + u) % 8

    def hop(direction, u, q):
        src = part.at[q, target(direction, u)] if (u == 1 or (u == 2 and q != direction)) else rr.at[direction, u - 2, q]
        return remote(
            src, rr.at[direction, u - 1, q],
            rs_s.at[direction, u - 1, q], rs_r.at[direction, u - 1, q], (right, left)[direction],
        )

    def spread(direction, t, q):
        origin = (z + 9 - t) % 8 if direction == 0 else (z + t - 1) % 8
        return remote(
            outs[q].at[origin], outs[q].at[origin],
            ag_s.at[direction, t - 1, q], ag_r.at[direction, t - 1, q], (right, left)[direction],
        )

    for direction in (0, 1):
        hop(direction, 1, direction).start()
    for direction in (0, 1):
        hop(direction, 2, 1 - direction).start()
    for u in (2, 3, 4):
        for q in (0, 1):
            for direction in (0, 1):
                if u == 2 and q != direction:
                    continue
                hop(direction, u - 1, q).wait_recv()
                add_into(rr.at[direction, u - 2, q], part.at[q, target(direction, u)])
                hop(direction, u, q).start()
    for q in (0, 1):
        hop(0, 4, q).wait_recv()
        hop(1, 4, q).wait_recv()
        total = rr[0, 3, q].astype(F32) + rr[1, 3, q].astype(F32) + part[q, z].astype(F32)
        total = total + (tokens, cots)[q][z].astype(F32)
        outs[q][z] = total.astype(BF)
        for direction in (0, 1):
            spread(direction, 1, q).start()
    for t in (2, 3, 4):
        for q in (0, 1):
            for direction in (0, 1):
                spread(direction, t - 1, q).wait_recv()
                if t < 4 or q == direction:
                    spread(direction, t, q).start()
    for direction in (0, 1):
        spread(direction, 4, direction).wait_recv()
    for direction in (0, 1):
        for u in (1, 2, 3, 4):
            for q in (0, 1):
                if u > 1 or q == direction:
                    hop(direction, u, q).wait_send()
                if u < 4 or q == direction:
                    spread(direction, u, q).wait_send()


def finish_call(part, tokens, cots):
    width = part.shape[3]
    shape = jax.ShapeDtypeStruct((8, 16, width), BF)
    return pl.pallas_call(
        finish_kernel,
        out_shape=(shape, shape),
        in_specs=[VMEM, VMEM, VMEM],
        out_specs=(VMEM, VMEM),
        scratch_shapes=[
            pltpu.VMEM((2, 4, 2, 16, width), BF),
            DMA((2, 4, 2)), DMA((2, 4, 2)), DMA((2, 4, 2)), DMA((2, 4, 2)),
        ],
        compiler_params=pltpu.CompilerParams(
            collective_id=3, has_side_effects=True, vmem_limit_bytes=40 * 1024 * 1024
        ),
    )(part, tokens.reshape(8, 16, width), cots.reshape(8, 16, width))


def shards(
    tokens,
    cotangent,
    dense_gate,
    dense_up,
    dense_down,
    expert_gate,
    expert_up,
    expert_down,
    expert_ids,
    route_weights,
):
    count, width = tokens.shape
    half = width // 2
    hid = dense_gate.shape[1]
    experts, cap = 16, 24
    y, x, c, z = place()

    flat_ids = expert_ids.reshape(-1)
    onehot = (flat_ids[:, None] == jnp.arange(experts, dtype=jnp.int32)[None, :]).astype(jnp.int32)
    earlier = jnp.cumsum(onehot, axis=0) - onehot
    placed = (flat_ids * cap + jnp.sum(earlier * onehot, axis=1)).reshape(count, 2)

    y_d = jnp.arange(4, dtype=jnp.int32)
    x_d = (x + z // 2 + 2 * ((y_d + y) % 2)) % 4
    e_d = (y_d % 2) * 8 + x_d * 2 + (c + z) % 2
    slots = (e_d[:, None] * cap + jnp.arange(cap, dtype=jnp.int32)[None, :]).reshape(-1)
    hits = slots[:, None, None] == placed[None, :, :]
    select = jnp.any(hits, axis=2).astype(BF)
    weighted = jnp.sum(jnp.where(hits, route_weights[None, :, :], 0.0), axis=2)
    slot_weight = jnp.sum(weighted, axis=1)

    low, high = slice(0, 2 * cap), slice(2 * cap, 4 * cap)

    def picked(values):
        return jnp.concatenate(
            [product(select[low], values[:, :half]), product(select[high], values[:, half:])], axis=0
        )

    send_rows = picked(tokens).astype(BF).reshape(4, cap, half)
    send_cots = (picked(cotangent) * slot_weight[:, None]).astype(BF).reshape(4, cap, half)
    send = jnp.concatenate([send_rows, send_cots], axis=1)
    dense_cat = jnp.concatenate([dense_gate, dense_up, dense_down.T], axis=1)
    recv, full = gather_call(send, dense_cat)

    gate, up, down = expert_gate[0], expert_up[0], expert_down[0]
    arrived = recv[:, :, :cap].reshape(-1, half)
    cots = recv[:, :, cap:].reshape(-1, half)
    mine = jnp.concatenate(
        [product(arrived, gate), product(arrived, up), times_transposed(cots, down)], axis=1
    )
    theirs = swap_call(mine.astype(BF).reshape(8, -1, 3 * hid)).reshape(-1, 3 * hid)

    full = full.reshape(width, 3 * hid)
    both = jnp.concatenate([tokens, cotangent], axis=0)
    dense_pre = product(both, full)
    active, slope = silu_pair(dense_pre[:count, :hid])
    pre_up = dense_pre[:count, hid : 2 * hid]
    grad_act = dense_pre[count:, 2 * hid :]
    zeros = jnp.zeros((count, hid), BF)
    spread = jnp.concatenate(
        [
            jnp.concatenate([zeros, zeros, (active * pre_up).astype(BF)], axis=1),
            jnp.concatenate(
                [(grad_act * pre_up * slope).astype(BF), (grad_act * active).astype(BF), zeros], axis=1
            ),
        ],
        axis=0,
    )
    dense_part = times_transposed(spread, full)
    swapped = jnp.concatenate([cotangent, tokens], axis=0)
    dw = transposed_times(swapped, spread).astype(BF).reshape(4, 4, 2, 112, 3 * hid)

    pre = mine + theirs.astype(F32)
    active, slope = silu_pair(pre[:, :hid])
    pre_up = pre[:, hid : 2 * hid]
    grad_act = pre[:, 2 * hid :]
    hidden = (active * pre_up).astype(BF)
    grad_gate = (grad_act * pre_up * slope).astype(BF)
    grad_up = (grad_act * active).astype(BF)
    back = (times_transposed(grad_gate, gate) + times_transposed(grad_up, up)).astype(BF)
    made = product(hidden, down).astype(BF)
    part = jnp.concatenate([back.reshape(8, 4, cap, half), made.reshape(8, 4, cap, half)], axis=2)
    ret, dense_grad = scatter_call(part, dw)

    place_back = select.reshape(2, 2 * cap, count)
    place_out = weighted.astype(BF).reshape(2, 2 * cap, count)
    ret_back = ret[:, :cap].reshape(2, 2 * cap, half)
    ret_out = ret[:, cap:].reshape(2, 2 * cap, half)
    moe_out = jnp.concatenate([transposed_times(place_out[h], ret_out[h]) for h in (0, 1)], axis=1)
    moe_back = jnp.concatenate([transposed_times(place_back[h], ret_back[h]) for h in (0, 1)], axis=1)
    total = jnp.stack([dense_part[:count] + moe_out, dense_part[count:] + moe_back]).astype(BF)
    output, input_grad = finish_call(total.reshape(2, 8, 16, width), tokens, cotangent)
    return (
        output.reshape(count, width),
        input_grad.reshape(count, width),
        dense_grad[:, :hid],
        dense_grad[:, hid : 2 * hid],
        dense_grad[:, 2 * hid :].T,
        transposed_times(arrived, grad_gate).astype(BF)[None],
        transposed_times(arrived, grad_up).astype(BF)[None],
        transposed_times(hidden, cots).astype(BF)[None],
    )


def solution(mesh):
    in_specs = (
        P(("dp", "expert"), None),
        P(("dp", "expert"), None),
        P(("dp", "expert"), "tensor"),
        P(("dp", "expert"), "tensor"),
        P("tensor", ("dp", "expert")),
        P("expert", "dp", "tensor"),
        P("expert", "dp", "tensor"),
        P("expert", "tensor", "dp"),
        P(("dp", "expert"), None),
        P(("dp", "expert"), None),
    )
    out_specs = (
        P(("dp", "expert"), None),
        P(("dp", "expert"), None),
        P(("dp", "expert"), "tensor"),
        P(("dp", "expert"), "tensor"),
        P("tensor", ("dp", "expert")),
        P("expert", "dp", "tensor"),
        P("expert", "dp", "tensor"),
        P("expert", "tensor", "dp"),
    )
    return jax.shard_map(shards, mesh=mesh, in_specs=in_specs, out_specs=out_specs, check_vma=False)
```

```python
import functools

import jax
import jax.numpy as jnp
from jax import lax
from jax.experimental import pallas as pl
from jax.experimental.pallas import tpu as pltpu
from jax.sharding import PartitionSpec as P

MESH = pl.DeviceIdType.MESH
BF = jnp.bfloat16
F32 = jnp.float32
HBM = pl.BlockSpec(memory_space=pl.ANY)
VMEM = pl.BlockSpec(memory_space=pltpu.VMEM)
DMA = pltpu.SemaphoreType.DMA
ROWS_A = pl.ds(0, 48)
ROWS_B = pl.ds(48, 64)


def silu_pair(values):
    logistic = jax.nn.sigmoid(values)
    return (values * logistic, logistic * (1.0 + values * (1.0 - logistic)))


def product(left, right):
    return jnp.dot(left, right, preferred_element_type=F32)


def times_transposed(left, right):
    return lax.dot_general(left, right, (((1,), (1,)), ((), ())), preferred_element_type=F32)


def transposed_times(left, right):
    return lax.dot_general(left, right, (((0,), (0,)), ((), ())), preferred_element_type=F32)


def place():
    dp, e, z = lax.axis_index("dp"), lax.axis_index("expert"), lax.axis_index("tensor")
    return dp * 2 + e // 8, (e // 2) % 4, e % 2, z


def device(y, x, c, z):
    return (y // 2, (y % 2) * 8 + x * 2 + c, z)


def dispatch_dest(y, x, c, z, j):
    return (y + j) % 4, (x + z // 2 + 2 * (j % 2)) % 4, (c + z) % 2


def dispatch_source(y, x, c, z, j):
    return (y + 4 - j) % 4, (x + 8 - z // 2 - 2 * (j % 2)) % 4, (c + z) % 2


def remote(src, dst, send_sem, recv_sem, dev):
    return pltpu.make_async_remote_copy(
        src_ref=src, dst_ref=dst, send_sem=send_sem, recv_sem=recv_sem, device_id=dev, device_id_type=MESH
    )


def greet(devices, conditional=()):
    barrier = pltpu.get_barrier_semaphore()
    for dev in devices:
        pl.semaphore_signal(barrier, inc=1, device_id=dev, device_id_type=MESH)
    for cond, dev in conditional:
        @pl.when(cond)
        def _():
            pl.semaphore_signal(barrier, inc=1, device_id=dev, device_id_type=MESH)
    count = jnp.int32(len(devices))
    for cond, dev in conditional:
        count = count + jnp.where(cond, jnp.int32(1), jnp.int32(0))
    pl.semaphore_wait(barrier, count)


def add_into(dst, *others):
    total = dst[...].astype(F32)
    for other in others:
        total = total + other[...].astype(F32)
    dst[...] = total.astype(BF)


ORDER = (0, -1, 1, -2, 2, -3, 3, 4)


def layer_kernel(
    send, w, gate, up, down, tokens, cots,
    ret, dgrad, ggrad, ugrad, lgrad, dpart,
    recv, full, cr, mine, theirs, via, acts, spread, part, rr, ra, rb, rc, rd,
    dsp_s, dsp_r, ag_s, ag_r, loc, da_s, da_r, near_s, near_r, far_s, far_r,
    ring_s, ring_r, ret_s, ret_r, d_s, d_r,
):
    y, x, c, z = place()
    hid = gate.shape[1]
    right, left = device(y, x, c, (z + 1) % 8), device(y, x, c, (z + 7) % 8)
    xi = [(x + i) % 4 for i in (1, 2, 3)]
    yi = [(y + i) % 4 for i in (1, 2, 3)]
    xs = [device(y, i, c, z) for i in xi]
    ys = [device(i, x, c, z) for i in yi]
    above, below = ys[0], ys[2]
    other = device(y, x, 1 - c, z)
    dests = [dispatch_dest(y, x, c, z, j) for j in range(4)]
    sources = [dispatch_source(y, x, c, z, j) for j in range(4)]
    greet(
        [device(*s, z) for s in sources[1:]] + [device(*d, z) for d in dests[1:]] + xs + ys + [other, left, right],
        [(z != 0, device(*sources[0], z)), (z != 0, device(*dests[0], z))],
    )


    def disp(j):
        return remote(send.at[(y + j) % 4], recv.at[z, y], dsp_s.at[j], dsp_r.at[j], device(*dests[j], z))

    here = pltpu.make_async_copy(send.at[y], recv.at[z, y], dsp_r.at[0])

    def carry(direction, t, j):
        origin = (z + 9 - t) % 8 if direction == 0 else (z + t - 1) % 8
        k = (y + 4 - j) % 4
        return remote(
            recv.at[origin, k], recv.at[origin, k],
            ag_s.at[direction, t - 1, j], ag_r.at[direction, t - 1, j], (right, left)[direction],
        )

    def carried(direction, t):
        return range(4) if t < 4 else ((0, 1), (2, 3))[direction]

    @pl.when(z == 0)
    def _():
        here.start()

    @pl.when(z != 0)
    def _():
        disp(0).start()

    for j in (1, 2, 3):
        disp(j).start()

    own = pltpu.make_async_copy(w, full.at[y, x, c], loc.at[0])
    own.start()
    one_a = [remote(w.at[ROWS_A], full.at[y, x, c, ROWS_A], da_s.at[0, i], da_r.at[0, i], xs[i]) for i in range(3)]
    one_b = [remote(w.at[ROWS_B], full.at[y, x, c, ROWS_B], da_s.at[1, i], da_r.at[1, i], ys[i]) for i in range(3)]
    two_a = [
        remote(full.at[y, :, c, ROWS_A], full.at[y, :, c, ROWS_A], da_s.at[2, i], da_r.at[2, i], ys[i])
        for i in range(3)
    ]
    two_b = [
        remote(full.at[:, x, c, ROWS_B], full.at[:, x, c, ROWS_B], da_s.at[3, i], da_r.at[3, i], xs[i])
        for i in range(3)
    ]
    three = [remote(full.at[i, :, c], full.at[i, :, c], da_s.at[4, i], da_r.at[4, i], other) for i in range(4)]
    for copy in one_a + one_b:
        copy.start()


    def block(r):
        return (z + 8 + ORDER[r]) % 8

    def near(r, h):
        return remote(
            mine.at[block(r), h], via.at[block(r), h], near_s.at[r, h], near_r.at[r, h], (above, below)[h]
        )

    def far(r, h):
        return remote(
            via.at[block(r), h], theirs.at[block(r), h], far_s.at[r, h], far_r.at[r, h], (above, below)[h]
        )

    def pre_block(r):
        b = block(r)
        rows = recv[b].reshape(192, recv.shape[3])
        results = (product(rows, gate[...]), product(rows, up[...]), times_transposed(rows, down[...]))
        for q in range(3):
            first = 24 if q == 2 else 0
            value = results[q].reshape(4, 48, hid)[:, first : first + 24].reshape(2, 48, hid)
            mine[b, :, q] = value.astype(BF)
        for h in (0, 1):
            near(r, h).start()

    def relay(r):
        for h in (0, 1):
            near(r, h).wait_recv()
            far(r, h).start()

    for j in range(4):
        if j == 0:
            @pl.when(z == 0)
            def _():
                here.wait()

            @pl.when(z != 0)
            def _():
                disp(0).wait_recv()
        else:
            disp(j).wait_recv()
        carry(0, 1, j).start()
        carry(1, 1, j).start()
    own.wait()
    for copy in one_a + one_b:
        copy.wait_recv()
    for copy in two_a + two_b:
        copy.start()
    pre_block(0)

    def carry_step(t):
        for j in range(4):
            for direction in (0, 1):
                carry(direction, t - 1, j).wait_recv()
                if j in carried(direction, t):
                    carry(direction, t, j).start()


    def dense_forward():
        both = jnp.concatenate([tokens[...], cots[...]], axis=0)
        pre = product(both, full[...].reshape(both.shape[1], 3 * hid))
        active, slope = silu_pair(pre[:128, :hid])
        pre_up = pre[:128, hid : 2 * hid]
        grad_act = pre[128:, 2 * hid :]
        zeros = jnp.zeros((128, hid), F32)
        spread[0:128, :] = jnp.concatenate([zeros, zeros, active * pre_up], axis=1).astype(BF)
        spread[128:256, :] = jnp.concatenate(
            [grad_act * pre_up * slope, grad_act * active, zeros], axis=1
        ).astype(BF)

        @pl.loop(0, 4)
        def _(i):
            rows = full[i].reshape(896, 3 * hid)
            dpart[:, pl.ds(pl.multiple_of(i * 896, 128), 896)] = times_transposed(spread[...], rows).astype(BF)

    def dense_weights():
        @pl.loop(0, 4)
        def _(i):
            cols = pl.ds(pl.multiple_of(i * 896, 128), 896)
            value = transposed_times(cots[:, cols], spread[0:128, :])
            value = value + transposed_times(tokens[:, cols], spread[128:256, :])
            full[i] = value.astype(BF).reshape(4, 2, 112, 3 * hid)

    carry_step(2)
    pre_block(1)
    pre_block(2)
    relay(0)
    for copy in two_a + two_b:
        copy.wait_recv()
    for copy in three:
        copy.start()
    carry_step(3)
    pre_block(3)
    pre_block(4)
    relay(1)
    relay(2)
    for copy in three:
        copy.wait_recv()
    dense_forward()
    carry_step(4)
    pre_block(5)
    pre_block(6)
    relay(3)
    relay(4)
    for copy in one_a + one_b + two_a + two_b + three:
        copy.wait_send()
    for direction in (0, 1):
        for j in carried(direction, 4):
            carry(direction, 4, j).wait_recv()
    pre_block(7)
    relay(5)
    relay(6)
    dense_weights()
    relay(7)


    def results_block(r):
        b = block(r)
        for h in (0, 1):
            far(r, h).wait_recv()
        pre = [mine[b, :, q].astype(F32) + theirs[b, :, q].astype(F32) for q in range(3)]
        active, slope = silu_pair(pre[0])
        zeros = jnp.zeros((4, 24, hid), F32)
        grad_gate = (pre[2] * pre[1] * slope).reshape(4, 24, hid)
        grad_up = (pre[2] * active).reshape(4, 24, hid)
        hidden = (active * pre[1]).reshape(4, 24, hid)
        acts[0, b] = jnp.concatenate([grad_gate, zeros], axis=1).astype(BF)
        acts[1, b] = jnp.concatenate([grad_up, zeros], axis=1).astype(BF)
        acts[2, b] = jnp.concatenate([zeros, hidden], axis=1).astype(BF)
        value = times_transposed(acts[0, b].reshape(192, hid), gate[...])
        value = value + times_transposed(acts[1, b].reshape(192, hid), up[...])
        value = value + product(acts[2, b].reshape(192, hid), down[...])
        part[b] = value.astype(BF).reshape(part.shape[1:])


    def target(direction, u):
        return (z + 5 - u) % 8 if direction == 0 else (z + 3 + u) % 8

    def members(direction, u):
        return range(4) if u > 1 else ((0, 1), (2, 3))[direction]

    def hop(direction, u, k):
        fresh = u == 1 or (u == 2 and k not in members(direction, 1))
        src = part.at[target(direction, u), k] if fresh else rr.at[direction, u - 2, k]
        return remote(
            src, rr.at[direction, u - 1, k],
            ring_s.at[direction, u - 1, k], ring_r.at[direction, u - 1, k], (right, left)[direction],
        )

    def ring_step(u):
        for k in range(4):
            for direction in (0, 1):
                if u == 2 and k not in members(direction, 1):
                    continue
                hop(direction, u - 1, k).wait_recv()
                add_into(rr.at[direction, u - 2, k], part.at[target(direction, u), k])
                hop(direction, u, k).start()


    d_one = [remote(full.at[i, :, 1 - c], cr.at[i], d_s.at[0, i], d_r.at[0, i], other) for i in range(4)]
    d_two_a = [remote(cr.at[yi[i], :, ROWS_A], ra.at[i], d_s.at[1, i], d_r.at[1, i], ys[i]) for i in range(3)]
    d_two_b = [remote(cr.at[:, xi[i], ROWS_B], rb.at[i], d_s.at[2, i], d_r.at[2, i], xs[i]) for i in range(3)]
    d_three_a = [remote(cr.at[y, xi[i], ROWS_A], rc.at[i], d_s.at[3, i], d_r.at[3, i], xs[i]) for i in range(3)]
    d_three_b = [remote(cr.at[yi[i], x, ROWS_B], rd.at[i], d_s.at[4, i], d_r.at[4, i], ys[i]) for i in range(3)]

    for copy in d_one:
        copy.start()
    results_block(7)
    for direction in (0, 1):
        for k in members(direction, 1):
            hop(direction, 1, k).start()
    results_block(5)
    results_block(6)
    for direction in (0, 1):
        for k in range(4):
            if k not in members(direction, 1):
                hop(direction, 2, k).start()
    for copy in d_one:
        copy.wait_recv()

    @pl.loop(0, 16)
    def _(i):
        add_into(cr.at[i // 4, i % 4], full.at[i // 4, i % 4, c])

    for copy in d_two_a + d_two_b:
        copy.start()
    ring_step(2)
    results_block(3)
    results_block(4)
    for copy in d_two_a + d_two_b:
        copy.wait_recv()

    @pl.loop(0, 4)
    def _(i):
        add_into(cr.at[y, i, ROWS_A], ra.at[0, i], ra.at[1, i], ra.at[2, i])
        add_into(cr.at[i, x, ROWS_B], rb.at[0, i], rb.at[1, i], rb.at[2, i])

    for copy in d_three_a + d_three_b:
        copy.start()
    ring_step(3)
    results_block(1)
    results_block(2)
    for copy in d_three_a + d_three_b:
        copy.wait_recv()
    add_into(cr.at[y, x, ROWS_A], rc.at[0], rc.at[1], rc.at[2])
    add_into(cr.at[y, x, ROWS_B], rd.at[0], rd.at[1], rd.at[2])
    dgrad[...] = cr[y, x]
    ring_step(4)
    results_block(0)


    @pl.loop(0, recv.shape[3] // 256)
    def _(i):
        cols = pl.ds(pl.multiple_of(i * 256, 256), 256)
        rows = recv[:, :, :, cols].reshape(1536, 256)
        ggrad[cols, :] = transposed_times(rows, acts[0].reshape(1536, hid)).astype(BF)
        ugrad[cols, :] = transposed_times(rows, acts[1].reshape(1536, hid)).astype(BF)
        lgrad[:, cols] = transposed_times(acts[2].reshape(1536, hid), rows).astype(BF)


    def home(j):
        return remote(
            rr.at[0, 3, (y + 4 - j) % 4], ret.at[y], ret_s.at[j], ret_r.at[j], device(*sources[j], z)
        )

    back = pltpu.make_async_copy(rr.at[0, 3, y], ret.at[y], ret_r.at[0])
    for k in range(4):
        hop(0, 4, k).wait_recv()
        hop(1, 4, k).wait_recv()
        add_into(rr.at[0, 3, k], rr.at[1, 3, k], part.at[z, k])

    @pl.when(z == 0)
    def _():
        back.start()

    @pl.when(z != 0)
    def _():
        home(0).start()

    for j in (1, 2, 3):
        home(j).start()

    @pl.when(z == 0)
    def _():
        back.wait()

    @pl.when(z != 0)
    def _():
        home(0).wait()
        disp(0).wait_send()

    for j in (1, 2, 3):
        home(j).wait()
        disp(j).wait_send()
    for direction in (0, 1):
        for t in (1, 2, 3, 4):
            for k in members(direction, t):
                hop(direction, t, k).wait_send()
            for j in carried(direction, t):
                carry(direction, t, j).wait_send()
    for r in range(8):
        for h in (0, 1):
            near(r, h).wait_send()
            far(r, h).wait_send()
    for copy in d_one + d_two_a + d_two_b + d_three_a + d_three_b:
        copy.wait_send()


def layer_call(send, w, gate, up, down, tokens, cots):
    half, hid = gate.shape
    lanes = w.shape[1]
    count, width = tokens.shape
    shape = jax.ShapeDtypeStruct
    swap = pltpu.VMEM((8, 2, 3, 48, hid), BF)
    rows = pltpu.VMEM((8, 4, 48, half), BF)
    return pl.pallas_call(
        layer_kernel,
        out_shape=(
            shape((4, 48, half), BF),
            shape((112, lanes), BF),
            shape((half, hid), BF),
            shape((half, hid), BF),
            shape((hid, half), BF),
            shape((2 * count, width), BF),
        ),
        in_specs=[HBM, HBM] + [VMEM] * 5,
        out_specs=(HBM,) + (VMEM,) * 5,
        scratch_shapes=[
            rows,
            pltpu.VMEM((4, 4, 2, 112, lanes), BF),
            pltpu.VMEM((4, 4, 112, lanes), BF),
            swap, swap, swap,
            pltpu.VMEM((3, 8, 4, 48, hid), BF),
            pltpu.VMEM((2 * count, lanes), BF),
            rows,
            pltpu.VMEM((2, 4, 4, 48, half), BF),
            pltpu.VMEM((3, 4, 48, lanes), BF),
            pltpu.VMEM((3, 4, 64, lanes), BF),
            pltpu.VMEM((3, 48, lanes), BF),
            pltpu.VMEM((3, 64, lanes), BF),
            DMA((4,)), DMA((4,)), DMA((2, 4, 4)), DMA((2, 4, 4)), DMA((1,)), DMA((5, 4)), DMA((5, 4)),
            DMA((8, 2)), DMA((8, 2)), DMA((8, 2)), DMA((8, 2)),
            DMA((2, 4, 4)), DMA((2, 4, 4)), DMA((4,)), DMA((4,)), DMA((5, 4)), DMA((5, 4)),
        ],
        compiler_params=pltpu.CompilerParams(
            collective_id=0, has_side_effects=True, vmem_limit_bytes=62 * 1024 * 1024
        ),
    )(send, w, gate, up, down, tokens, cots)


def finish_kernel(part, tokens, cots, out, back, rr, rs_s, rs_r, ag_s, ag_r):
    y, x, c, z = place()
    right, left = device(y, x, c, (z + 1) % 8), device(y, x, c, (z + 7) % 8)
    greet([left, right])
    outs = (out, back)

    def target(direction, u):
        return (z + 5 - u) % 8 if direction == 0 else (z + 3 + u) % 8

    def hop(direction, u, q):
        src = part.at[q, target(direction, u)] if (u == 1 or (u == 2 and q != direction)) else rr.at[direction, u - 2, q]
        return remote(
            src, rr.at[direction, u - 1, q],
            rs_s.at[direction, u - 1, q], rs_r.at[direction, u - 1, q], (right, left)[direction],
        )

    def spread(direction, t, q):
        origin = (z + 9 - t) % 8 if direction == 0 else (z + t - 1) % 8
        return remote(
            outs[q].at[origin], outs[q].at[origin],
            ag_s.at[direction, t - 1, q], ag_r.at[direction, t - 1, q], (right, left)[direction],
        )

    for direction in (0, 1):
        hop(direction, 1, direction).start()
    for direction in (0, 1):
        hop(direction, 2, 1 - direction).start()
    for u in (2, 3, 4):
        for q in (0, 1):
            for direction in (0, 1):
                if u == 2 and q != direction:
                    continue
                hop(direction, u - 1, q).wait_recv()
                add_into(rr.at[direction, u - 2, q], part.at[q, target(direction, u)])
                hop(direction, u, q).start()
    for q in (0, 1):
        hop(0, 4, q).wait_recv()
        hop(1, 4, q).wait_recv()
        total = rr[0, 3, q].astype(F32) + rr[1, 3, q].astype(F32) + part[q, z].astype(F32)
        total = total + (tokens, cots)[q][z].astype(F32)
        outs[q][z] = total.astype(BF)
        for direction in (0, 1):
            spread(direction, 1, q).start()
    for t in (2, 3, 4):
        for q in (0, 1):
            for direction in (0, 1):
                spread(direction, t - 1, q).wait_recv()
                if t < 4 or q == direction:
                    spread(direction, t, q).start()
    for direction in (0, 1):
        spread(direction, 4, direction).wait_recv()
    for direction in (0, 1):
        for u in (1, 2, 3, 4):
            for q in (0, 1):
                if u > 1 or q == direction:
                    hop(direction, u, q).wait_send()
                if u < 4 or q == direction:
                    spread(direction, u, q).wait_send()


def finish_call(part, tokens, cots):
    width = part.shape[3]
    shape = jax.ShapeDtypeStruct((8, 16, width), BF)
    return pl.pallas_call(
        finish_kernel,
        out_shape=(shape, shape),
        in_specs=[VMEM, VMEM, VMEM],
        out_specs=(VMEM, VMEM),
        scratch_shapes=[
            pltpu.VMEM((2, 4, 2, 16, width), BF),
            DMA((2, 4, 2)), DMA((2, 4, 2)), DMA((2, 4, 2)), DMA((2, 4, 2)),
        ],
        compiler_params=pltpu.CompilerParams(
            collective_id=3, has_side_effects=True, vmem_limit_bytes=40 * 1024 * 1024
        ),
    )(part, tokens.reshape(8, 16, width), cots.reshape(8, 16, width))


def shards(
    tokens,
    cotangent,
    dense_gate,
    dense_up,
    dense_down,
    expert_gate,
    expert_up,
    expert_down,
    expert_ids,
    route_weights,
):
    count, width = tokens.shape
    half = width // 2
    hid = dense_gate.shape[1]
    experts, cap = 16, 24
    y, x, c, z = place()

    flat_ids = expert_ids.reshape(-1)
    onehot = (flat_ids[:, None] == jnp.arange(experts, dtype=jnp.int32)[None, :]).astype(jnp.int32)
    earlier = jnp.cumsum(onehot, axis=0) - onehot
    placed = (flat_ids * cap + jnp.sum(earlier * onehot, axis=1)).reshape(count, 2)

    y_d = jnp.arange(4, dtype=jnp.int32)
    x_d = (x + z // 2 + 2 * ((y_d + y) % 2)) % 4
    e_d = (y_d % 2) * 8 + x_d * 2 + (c + z) % 2
    slots = (e_d[:, None] * cap + jnp.arange(cap, dtype=jnp.int32)[None, :]).reshape(-1)
    hits = slots[:, None, None] == placed[None, :, :]
    select = jnp.any(hits, axis=2).astype(BF)
    weighted = jnp.sum(jnp.where(hits, route_weights[None, :, :], 0.0), axis=2)
    slot_weight = jnp.sum(weighted, axis=1)

    low, high = slice(0, 2 * cap), slice(2 * cap, 4 * cap)

    def picked(values):
        return jnp.concatenate(
            [product(select[low], values[:, :half]), product(select[high], values[:, half:])], axis=0
        )

    send_rows = picked(tokens).astype(BF).reshape(4, cap, half)
    send_cots = (picked(cotangent) * slot_weight[:, None]).astype(BF).reshape(4, cap, half)
    send = jnp.concatenate([send_rows, send_cots], axis=1)
    dense_cat = jnp.concatenate([dense_gate, dense_up, dense_down.T], axis=1)
    ret, dense_grad, gate_grad, up_grad, down_grad, dense_part = layer_call(
        send, dense_cat, expert_gate[0], expert_up[0], expert_down[0], tokens, cotangent
    )

    place_back = select.reshape(2, 2 * cap, count)
    place_out = weighted.astype(BF).reshape(2, 2 * cap, count)
    ret_back = ret[:, :cap].reshape(2, 2 * cap, half)
    ret_out = ret[:, cap:].reshape(2, 2 * cap, half)
    moe_out = jnp.concatenate([transposed_times(place_out[h], ret_out[h]) for h in (0, 1)], axis=1)
    moe_back = jnp.concatenate([transposed_times(place_back[h], ret_back[h]) for h in (0, 1)], axis=1)
    total = (dense_part.astype(F32).reshape(2, count, width) + jnp.stack([moe_out, moe_back])).astype(BF)
    output, input_grad = finish_call(total.reshape(2, 8, 16, width), tokens, cotangent)
    return (
        output.reshape(count, width),
        input_grad.reshape(count, width),
        dense_grad[:, :hid],
        dense_grad[:, hid : 2 * hid],
        dense_grad[:, 2 * hid :].T,
        gate_grad[None],
        up_grad[None],
        down_grad[None],
    )


def solution(mesh):
    in_specs = (
        P(("dp", "expert"), None),
        P(("dp", "expert"), None),
        P(("dp", "expert"), "tensor"),
        P(("dp", "expert"), "tensor"),
        P("tensor", ("dp", "expert")),
        P("expert", "dp", "tensor"),
        P("expert", "dp", "tensor"),
        P("expert", "tensor", "dp"),
        P(("dp", "expert"), None),
        P(("dp", "expert"), None),
    )
    out_specs = (
        P(("dp", "expert"), None),
        P(("dp", "expert"), None),
        P(("dp", "expert"), "tensor"),
        P(("dp", "expert"), "tensor"),
        P("tensor", ("dp", "expert")),
        P("expert", "dp", "tensor"),
        P("expert", "dp", "tensor"),
        P("expert", "tensor", "dp"),
    )
    return jax.shard_map(shards, mesh=mesh, in_specs=in_specs, out_specs=out_specs, check_vma=False)
```

```python
import functools

import jax
import jax.numpy as jnp
from jax import lax
from jax.experimental import pallas as pl
from jax.experimental.pallas import tpu as pltpu
from jax.sharding import PartitionSpec as P

MESH = pl.DeviceIdType.MESH
BF = jnp.bfloat16
F32 = jnp.float32
HBM = pl.BlockSpec(memory_space=pl.ANY)
VMEM = pl.BlockSpec(memory_space=pltpu.VMEM)
DMA = pltpu.SemaphoreType.DMA
ROWS_A = pl.ds(0, 48)
ROWS_B = pl.ds(48, 64)
ROWS_A0, ROWS_A1 = pl.ds(0, 16), pl.ds(16, 32)
ROWS_B0, ROWS_B1 = pl.ds(48, 32), pl.ds(80, 32)
LOW, HIGH = pl.ds(0, 2), pl.ds(2, 2)


def silu_pair(values):
    logistic = jax.nn.sigmoid(values)
    return (values * logistic, logistic * (1.0 + values * (1.0 - logistic)))


def product(left, right):
    return jnp.dot(left, right, preferred_element_type=F32)


def times_transposed(left, right):
    return lax.dot_general(left, right, (((1,), (1,)), ((), ())), preferred_element_type=F32)


def transposed_times(left, right):
    return lax.dot_general(left, right, (((0,), (0,)), ((), ())), preferred_element_type=F32)


def place():
    dp, e, z = lax.axis_index("dp"), lax.axis_index("expert"), lax.axis_index("tensor")
    return dp * 2 + e // 8, (e // 2) % 4, e % 2, z


def device(y, x, c, z):
    return (y // 2, (y % 2) * 8 + x * 2 + c, z)


def dispatch_dest(y, x, c, owner, j):
    return (y + j) % 4, (x + owner // 2 + 2 * (j % 2)) % 4, (c + owner) % 2


def dispatch_source(y, x, c, owner, j):
    return (y + 4 - j) % 4, (x + 8 - owner // 2 - 2 * (j % 2)) % 4, (c + owner) % 2


def remote(src, dst, send_sem, recv_sem, dev):
    return pltpu.make_async_remote_copy(
        src_ref=src, dst_ref=dst, send_sem=send_sem, recv_sem=recv_sem, device_id=dev, device_id_type=MESH
    )


def greet(devices, conditional=()):
    barrier = pltpu.get_barrier_semaphore()
    for dev in devices:
        pl.semaphore_signal(barrier, inc=1, device_id=dev, device_id_type=MESH)
    for cond, dev in conditional:
        @pl.when(cond)
        def _():
            pl.semaphore_signal(barrier, inc=1, device_id=dev, device_id_type=MESH)
    count = jnp.int32(len(devices))
    for cond, dev in conditional:
        count = count + jnp.where(cond, jnp.int32(1), jnp.int32(0))
    pl.semaphore_wait(barrier, count)


def add_into(dst, *others):
    total = dst[...].astype(F32)
    for other in others:
        total = total + other[...].astype(F32)
    dst[...] = total.astype(BF)


ORDER = (0, 3, -3, 4, -1, 1, -2, 2)
DIRECT = 3
HOME = (0, 3)


def layer_kernel(
    sel, slot, tokens, cots, w, gate, up, down,
    back, out, dgrad, wgrad,
    send, wt, recv, full, cr, mine, theirs, via, acts, spread, part, rr, ra, rb, rc, rd, ret, tot, rz,
    wt_s, dsp_s, dsp_r, ag_s, ag_r, loc, da_s, da_r, near_s, near_r, far_s, far_r,
    ring_s, ring_r, ret_s, ret_r, d_s, d_r, rs_s, rs_r, fin_s, fin_r,
):
    y, x, c, z = place()
    hid, half = gate.shape
    right, left = device(y, x, c, (z + 1) % 8), device(y, x, c, (z + 7) % 8)
    xp, xm, yp, ym = (x + 1) % 4, (x + 3) % 4, (y + 1) % 4, (y + 3) % 4
    east, west = device(y, xp, c, z), device(y, xm, c, z)
    above, below = device(yp, x, c, z), device(ym, x, c, z)
    other = device(y, x, 1 - c, z)

    def block(r):
        return (z + 8 + ORDER[r]) % 8

    def dest(r, j):
        return device(*dispatch_dest(y, x, c, block(r), j), z)

    def source(r, j):
        return device(*dispatch_source(y, x, c, block(r), j), z)

    greet(
        [source(r, j) for r in range(DIRECT) for j in (1, 2, 3)]
        + [dest(r, j) for r in HOME for j in (1, 2, 3)]
        + [east, west, above, below, other, left, right],
        [(block(r) != 0, source(r, 0)) for r in range(DIRECT)] + [(block(r) != 0, dest(r, 0)) for r in HOME],
    )
    weights = [
        pltpu.make_async_copy(ref, wt.at[pl.ds(i * hid, hid)], wt_s.at[i]) for i, ref in enumerate((gate, up, down))
    ]
    for copy in weights:
        copy.start()


    def build(r):
        for h in (0, 1):
            cols = slice(h * half, (h + 1) * half)
            chosen = sel[h, r].reshape(96, 256)
            value = product(chosen[:, :128], tokens[:, cols]) + product(chosen[:, 128:], cots[:, cols])
            send[h, r] = (value * slot[h, r].reshape(96, 1)).astype(BF).reshape(2, 48, half)

    def straight(j, r, src, dst, send_sem, recv_sem, dev, action):
        copy = remote(src, dst, send_sem, recv_sem, dev)
        if j:
            getattr(copy, action)()
            return

        @pl.when(block(r) == 0)
        def _():
            if action != "wait_send":
                stay = pltpu.make_async_copy(src, dst, recv_sem)
                stay.start() if action == "start" else stay.wait()

        @pl.when(block(r) != 0)
        def _():
            getattr(copy, action)()

    def disp(r, j, action):
        y_d = (y + j) % 4
        straight(
            j, r, send.at[y_d // 2, r, y_d % 2], recv.at[block(r), y], dsp_s.at[r, j], dsp_r.at[r, j], dest(r, j), action
        )

    def carried(direction, t):
        return range(4) if t < 3 else ((0, 1), (2, 3))[direction]

    def carry_step(t):
        for j in range(4):
            for direction in (0, 1):
                carry(direction, t - 1, j).wait_recv()
                if j in carried(direction, t):
                    carry(direction, t, j).start()

    def carry(direction, t, j):
        ahead = t if t < 3 else 4
        origin = (z + 9 - ahead) % 8 if direction == 0 else (z + ahead - 1) % 8
        k = (y + 4 - j) % 4
        return remote(
            recv.at[origin, k], recv.at[origin, k],
            ag_s.at[direction, t - 1, j], ag_r.at[direction, t - 1, j], (right, left)[direction],
        )

    build(0)
    for j in range(4):
        disp(0, j, "start")
    for r in range(1, DIRECT):
        build(r)


    own = pltpu.make_async_copy(w, full.at[y, x, c], loc.at[0])
    own.start()

    def pass_on(stage, i, place_of, dev):
        return remote(place_of, place_of, da_s.at[stage, i], da_r.at[stage, i], dev)

    def first_send(i, rows, dev):
        return remote(w.at[rows], full.at[y, x, c, rows], da_s.at[0, i], da_r.at[0, i], dev)

    ga = [
        first_send(0, ROWS_A, east),
        first_send(1, ROWS_A, west),
        first_send(2, ROWS_B, above),
        first_send(3, ROWS_B, below),
    ]
    gb = [
        pass_on(1, 0, full.at[y, xm, c, ROWS_A0], east),
        pass_on(1, 1, full.at[y, xp, c, ROWS_A1], west),
        pass_on(1, 2, full.at[ym, x, c, ROWS_B0], above),
        pass_on(1, 3, full.at[yp, x, c, ROWS_B1], below),
    ]
    gc = [
        pass_on(2, 0, full.at[y, :, c, ROWS_A], above),
        pass_on(2, 1, full.at[y, :, c, ROWS_A], below),
        pass_on(2, 2, full.at[:, x, c, ROWS_B], east),
        pass_on(2, 3, full.at[:, x, c, ROWS_B], west),
    ]
    gd = [
        pass_on(3, 0, full.at[ym, LOW, c, ROWS_A], above),
        pass_on(3, 1, full.at[yp, HIGH, c, ROWS_A], below),
        pass_on(3, 2, full.at[LOW, xm, c, ROWS_B], east),
        pass_on(3, 3, full.at[HIGH, xp, c, ROWS_B], west),
    ]
    ge = [pass_on(4, i, full.at[i, :, c], other) for i in range(4)]

    def after(earlier, later):
        for copy in earlier:
            copy.wait_recv()
        for copy in later:
            copy.start()


    def near(r, h):
        return remote(
            mine.at[block(r), h], via.at[block(r), h], near_s.at[r, h], near_r.at[r, h], (above, below)[h]
        )

    def far(r, h):
        return remote(
            via.at[block(r), h], theirs.at[block(r), h], far_s.at[r, h], far_r.at[r, h], (above, below)[h]
        )

    def pre_block(r):
        b = block(r)
        value = times_transposed(recv[b].reshape(192, half), wt[...]).reshape(4, 48, 3 * hid)
        lane = lax.broadcasted_iota(jnp.int32, (4, 24, 3 * hid), 2)
        value = jnp.where(lane < 2 * hid, value[:, :24], value[:, 24:])
        mine[b] = value.reshape(2, 48, 3 * hid).astype(BF)
        for h in (0, 1):
            near(r, h).start()

    def relay(r):
        for h in (0, 1):
            near(r, h).wait_recv()
            far(r, h).start()


    def results_block(r):
        b = block(r)
        for h in (0, 1):
            far(r, h).wait_recv()
        pre = (mine[b].astype(F32) + theirs[b].astype(F32)).reshape(4, 24, 3 * hid)
        pre_up, grad_act = pre[:, :, hid : 2 * hid], pre[:, :, 2 * hid :]
        active, slope = silu_pair(pre[:, :, :hid])
        zeros = jnp.zeros((4, 24, hid), F32)
        first = jnp.concatenate([grad_act * pre_up * slope, grad_act * active, zeros], axis=2)
        second = jnp.concatenate([zeros, zeros, active * pre_up], axis=2)
        acts[b] = jnp.concatenate([first, second], axis=1).astype(BF)
        part[b] = product(acts[b].reshape(192, 3 * hid), wt[...]).astype(BF).reshape(4, 48, half)


    def dense_forward():
        both = jnp.concatenate([tokens[...], cots[...]], axis=0)
        pre = product(both, full[...].reshape(both.shape[1], 3 * hid))
        active, slope = silu_pair(pre[:128, :hid])
        pre_up = pre[:128, hid : 2 * hid]
        grad_act = pre[128:, 2 * hid :]
        zeros = jnp.zeros((128, hid), F32)
        spread[0:128, :] = jnp.concatenate(
            [grad_act * pre_up * slope, grad_act * active, zeros], axis=1
        ).astype(BF)
        spread[128:256, :] = jnp.concatenate([zeros, zeros, active * pre_up], axis=1).astype(BF)

        @pl.loop(0, 4)
        def _(i):
            rows = full[i].reshape(896, 3 * hid)
            value = times_transposed(spread[...], rows).astype(BF)
            tot[:, :, :, pl.ds(pl.multiple_of(i * 896, 128), 896)] = value.reshape(2, 8, 16, 896)

    def dense_weights():
        @pl.loop(0, 4)
        def _(i):
            cols = pl.ds(pl.multiple_of(i * 896, 128), 896)
            value = transposed_times(tokens[:, cols], spread[0:128, :])
            value = value + transposed_times(cots[:, cols], spread[128:256, :])
            full[i] = value.astype(BF).reshape(4, 2, 112, 3 * hid)


    def target(direction, v):
        return (z + 4 - v) % 8 if direction == 0 else (z + 4 + v) % 8

    def hop(direction, v, k):
        src = part.at[target(direction, 1), k] if v == 1 else rr.at[direction, v - 2, k]
        return remote(
            src, rr.at[direction, v - 1, k],
            ring_s.at[direction, v - 1, k], ring_r.at[direction, v - 1, k], (right, left)[direction],
        )

    def ring_step(v):
        for k in range(4):
            for direction in (0, 1):
                hop(direction, v - 1, k).wait_recv()
                add_into(rr.at[direction, v - 2, k], part.at[target(direction, v), k])
                hop(direction, v, k).start()

    def home(r, j, action):
        k = (y + 4 - j) % 4
        src = rr.at[0, 2, k] if r == 0 else part.at[block(r), k]
        straight(j, r, src, ret.at[r // 3, y], ret_s.at[r // 3, j], ret_r.at[r // 3, j], source(r, j), action)


    def partial(stage, i, src, dst, dev):
        return remote(src, dst, d_s.at[stage, i], d_r.at[stage, i], dev)

    yo, xo = (y + 2) % 4, (x + 2) % 4
    s_one = [partial(0, i, full.at[i, :, 1 - c], cr.at[i], other) for i in range(4)]
    s_two = [
        partial(1, 0, cr.at[yo, LOW, ROWS_A], ra.at[0, LOW], above),
        partial(1, 1, cr.at[yo, HIGH, ROWS_A], ra.at[0, HIGH], below),
        partial(1, 2, cr.at[LOW, xo, ROWS_B], rb.at[0, LOW], east),
        partial(1, 3, cr.at[HIGH, xo, ROWS_B], rb.at[0, HIGH], west),
    ]
    s_three = [
        partial(2, 0, cr.at[yp, :, ROWS_A], ra.at[1], above),
        partial(2, 1, cr.at[ym, :, ROWS_A], ra.at[2], below),
        partial(2, 2, cr.at[:, xp, ROWS_B], rb.at[1], east),
        partial(2, 3, cr.at[:, xm, ROWS_B], rb.at[2], west),
    ]
    s_four = [
        partial(3, 0, cr.at[y, xo, ROWS_A0], rc.at[0, ROWS_A0], east),
        partial(3, 1, cr.at[y, xo, ROWS_A1], rc.at[0, ROWS_A1], west),
        partial(3, 2, cr.at[yo, x, ROWS_B0], rd.at[0, pl.ds(0, 32)], above),
        partial(3, 3, cr.at[yo, x, ROWS_B1], rd.at[0, pl.ds(32, 32)], below),
    ]
    s_five = [
        partial(4, 0, cr.at[y, xp, ROWS_A], rc.at[1], east),
        partial(4, 1, cr.at[y, xm, ROWS_A], rc.at[2], west),
        partial(4, 2, cr.at[yp, x, ROWS_B], rd.at[1], above),
        partial(4, 3, cr.at[ym, x, ROWS_B], rd.at[2], below),
    ]

    def scatter_two():
        for copy in s_one:
            copy.wait_recv()

        @pl.loop(0, 16)
        def _(i):
            add_into(cr.at[i // 4, i % 4], full.at[i // 4, i % 4, c])

        for copy in s_two:
            copy.start()

    def scatter_three():
        for copy in s_two:
            copy.wait_recv()

        @pl.loop(0, 2)
        def _(i):
            add_into(cr.at[yp, i, ROWS_A], ra.at[0, i])
            add_into(cr.at[ym, i + 2, ROWS_A], ra.at[0, i + 2])
            add_into(cr.at[i, xp, ROWS_B], rb.at[0, i])
            add_into(cr.at[i + 2, xm, ROWS_B], rb.at[0, i + 2])

        for copy in s_three:
            copy.start()

    def scatter_four():
        for copy in s_three:
            copy.wait_recv()

        @pl.loop(0, 4)
        def _(i):
            add_into(cr.at[y, i, ROWS_A], ra.at[1, i], ra.at[2, i])
            add_into(cr.at[i, x, ROWS_B], rb.at[1, i], rb.at[2, i])

        for copy in s_four:
            copy.start()

    def scatter_five():
        for copy in s_four:
            copy.wait_recv()
        add_into(cr.at[y, xp, ROWS_A0], rc.at[0, ROWS_A0])
        add_into(cr.at[y, xm, ROWS_A1], rc.at[0, ROWS_A1])
        add_into(cr.at[yp, x, ROWS_B0], rd.at[0, pl.ds(0, 32)])
        add_into(cr.at[ym, x, ROWS_B1], rd.at[0, pl.ds(32, 32)])
        for copy in s_five:
            copy.start()

    def scatter_end():
        for copy in s_five:
            copy.wait_recv()
        add_into(cr.at[y, x, ROWS_A], rc.at[1], rc.at[2])
        add_into(cr.at[y, x, ROWS_B], rd.at[1], rd.at[2])
        dgrad[...] = cr[y, x]


    def expert_weights(first, count):
        rows = acts[:, :, :, first : first + count].reshape(1536, count)
        wgrad[first : first + count, :] = transposed_times(rows, recv[...].reshape(1536, half)).astype(BF)


    outs = (back, out)

    def final_target(direction, u):
        return (z + 5 - u) % 8 if direction == 0 else (z + 3 + u) % 8

    def final_hop(direction, u, q):
        fresh = u == 1 or (u == 2 and q != direction)
        src = tot.at[q, final_target(direction, u)] if fresh else rz.at[direction, u - 2, q]
        return remote(
            src, rz.at[direction, u - 1, q],
            rs_s.at[direction, u - 1, q], rs_r.at[direction, u - 1, q], (right, left)[direction],
        )

    def final_step(u):
        for q in (0, 1):
            for direction in (0, 1):
                if u == 2 and q != direction:
                    continue
                final_hop(direction, u - 1, q).wait_recv()
                add_into(rz.at[direction, u - 2, q], tot.at[q, final_target(direction, u)])
                final_hop(direction, u, q).start()

    def share(direction, t, q):
        origin = (z + 9 - t) % 8 if direction == 0 else (z + t - 1) % 8
        return remote(
            outs[q].at[origin], outs[q].at[origin],
            fin_s.at[direction, t - 1, q], fin_r.at[direction, t - 1, q], (right, left)[direction],
        )


    for j in range(4):
        disp(0, j, "wait_recv")
        carry(0, 1, j).start()
        carry(1, 1, j).start()
    for r in range(1, DIRECT):
        for j in range(4):
            disp(r, j, "start")
    for copy in ga:
        copy.start()
    for copy in weights:
        copy.wait()
    pre_block(0)
    carry_step(2)
    after(ga, gb)
    for r in range(1, DIRECT):
        for j in range(4):
            disp(r, j, "wait_recv")
        pre_block(r)
    relay(0)
    pre_block(4)
    pre_block(5)
    own.wait()
    after(gb, gc)
    relay(1)
    relay(2)
    carry_step(3)
    for r in (1, 2):
        results_block(r)
        for k in range(4):
            hop(r - 1, 1, k).start()
    pre_block(6)
    pre_block(7)
    relay(4)
    relay(5)
    after(gc, gd)
    relay(6)
    relay(7)
    for direction in (0, 1):
        for j in carried(direction, 3):
            carry(direction, 3, j).wait_recv()
    pre_block(3)
    results_block(6)
    results_block(7)
    relay(3)
    ring_step(2)
    after(gd, ge)
    results_block(3)
    for j in range(4):
        home(3, j, "start")
    results_block(4)
    results_block(5)
    after(ge, ())
    dense_forward()
    ring_step(3)
    results_block(0)
    for copy in ga + gb + gc + gd + ge:
        copy.wait_send()
    dense_weights()
    for copy in s_one:
        copy.start()
    for k in range(4):
        hop(0, 3, k).wait_recv()
        hop(1, 3, k).wait_recv()
        add_into(rr.at[0, 2, k], rr.at[1, 2, k], part.at[z, k])
    for j in range(4):
        home(0, j, "start")
    scatter_two()
    expert_weights(0, 256)
    scatter_three()
    for i in range(1, 3):
        expert_weights(256 * i, 256)
    expert_weights(768, 3 * hid - 768)
    for r in HOME:
        for j in range(4):
            home(r, j, "wait_recv")
    for h in (0, 1):
        cols = slice(h * half, (h + 1) * half)
        value = jnp.zeros((256, half), F32)
        for i, r in enumerate(HOME):
            rows = ret[i, 2 * h : 2 * h + 2].reshape(96, half).astype(F32) * slot[h, r].reshape(96, 1)
            value = value + transposed_times(sel[h, r].reshape(96, 256), rows.astype(BF))
        value = value.reshape(2, 8, 16, half)
        tot[:, :, :, cols] = (tot[:, :, :, cols].astype(F32) + value).astype(BF)
    for direction in (0, 1):
        final_hop(direction, 1, direction).start()
    for direction in (0, 1):
        final_hop(direction, 2, 1 - direction).start()
    scatter_four()
    final_step(2)
    scatter_five()
    final_step(3)
    final_step(4)
    scatter_end()
    mine_rows = pl.ds(pl.multiple_of(z * 16, 16), 16)
    for q in (0, 1):
        final_hop(0, 4, q).wait_recv()
        final_hop(1, 4, q).wait_recv()
        total = rz[0, 3, q].astype(F32) + rz[1, 3, q].astype(F32) + tot[q, z].astype(F32)
        total = total + (cots, tokens)[q][mine_rows, :].astype(F32)
        outs[q][z] = total.astype(BF)
        for direction in (0, 1):
            share(direction, 1, q).start()
    for t in (2, 3, 4):
        for q in (0, 1):
            for direction in (0, 1):
                share(direction, t - 1, q).wait_recv()
                if t < 4 or q == direction:
                    share(direction, t, q).start()
    for direction in (0, 1):
        share(direction, 4, direction).wait_recv()


    for r in range(DIRECT):
        for j in range(4):
            disp(r, j, "wait_send")
    for r in HOME:
        for j in range(4):
            home(r, j, "wait_send")
    for r in range(8):
        for h in (0, 1):
            near(r, h).wait_send()
            far(r, h).wait_send()
    for direction in (0, 1):
        for k in range(4):
            for t in (1, 2, 3):
                if k in carried(direction, t):
                    carry(direction, t, k).wait_send()
            for v in (1, 2, 3):
                hop(direction, v, k).wait_send()
        for u in (1, 2, 3, 4):
            for q in (0, 1):
                if u > 1 or q == direction:
                    final_hop(direction, u, q).wait_send()
                if u < 4 or q == direction:
                    share(direction, u, q).wait_send()
    for copy in s_one + s_two + s_three + s_four + s_five:
        copy.wait_send()


def layer_call(sel, slot, tokens, cots, w, gate, up, down):
    hid, half = gate.shape
    lanes = w.shape[1]
    count, width = tokens.shape
    shape = jax.ShapeDtypeStruct
    swap = pltpu.VMEM((8, 2, 48, lanes), BF)
    rows = pltpu.VMEM((8, 4, 48, half), BF)
    return pl.pallas_call(
        layer_kernel,
        out_shape=(
            shape((8, 16, width), BF),
            shape((8, 16, width), BF),
            shape((112, lanes), BF),
            shape((lanes, half), BF),
        ),
        in_specs=[VMEM] * 4 + [HBM] * 4,
        out_specs=(VMEM,) * 4,
        scratch_shapes=[
            pltpu.VMEM((2, DIRECT, 2, 48, half), BF),
            pltpu.VMEM((lanes, half), BF),
            rows,
            pltpu.VMEM((4, 4, 2, 112, lanes), BF),
            pltpu.VMEM((4, 4, 112, lanes), BF),
            swap, swap, swap,
            pltpu.VMEM((8, 4, 48, lanes), BF),
            pltpu.VMEM((2 * count, lanes), BF),
            rows,
            pltpu.VMEM((2, 3, 4, 48, half), BF),
            pltpu.VMEM((3, 4, 48, lanes), BF),
            pltpu.VMEM((3, 4, 64, lanes), BF),
            pltpu.VMEM((3, 48, lanes), BF),
            pltpu.VMEM((3, 64, lanes), BF),
            pltpu.VMEM((len(HOME), 4, 48, half), BF),
            pltpu.VMEM((2, 8, 16, width), BF),
            pltpu.VMEM((2, 4, 2, 16, width), BF),
            DMA((3,)), DMA((DIRECT, 4)), DMA((DIRECT, 4)), DMA((2, 3, 4)), DMA((2, 3, 4)), DMA((1,)),
            DMA((5, 4)), DMA((5, 4)),
            DMA((8, 2)), DMA((8, 2)), DMA((8, 2)), DMA((8, 2)),
            DMA((2, 3, 4)), DMA((2, 3, 4)), DMA((len(HOME), 4)), DMA((len(HOME), 4)), DMA((5, 4)), DMA((5, 4)),
            DMA((2, 4, 2)), DMA((2, 4, 2)), DMA((2, 4, 2)), DMA((2, 4, 2)),
        ],
        compiler_params=pltpu.CompilerParams(
            collective_id=0, has_side_effects=True, vmem_limit_bytes=63 * 1024 * 1024
        ),
    )(sel, slot, tokens, cots, w, gate, up, down)


def shards(
    tokens,
    cotangent,
    dense_gate,
    dense_up,
    dense_down,
    expert_gate,
    expert_up,
    expert_down,
    expert_ids,
    route_weights,
):
    count, width = tokens.shape
    hid = dense_gate.shape[1]
    experts, cap = 16, 24
    y, x, c, z = place()

    flat_ids = expert_ids.reshape(-1)
    onehot = (flat_ids[:, None] == jnp.arange(experts, dtype=jnp.int32)[None, :]).astype(jnp.int32)
    earlier = jnp.cumsum(onehot, axis=0) - onehot
    placed = (flat_ids * cap + jnp.sum(earlier * onehot, axis=1)).reshape(count, 2)

    owner = (z + 8 + jnp.array(ORDER[:4], jnp.int32)) % 8
    y_d = jnp.arange(4, dtype=jnp.int32).reshape(2, 1, 2)
    x_d = (x + owner[None, :, None] // 2 + 2 * ((y_d + y) % 2)) % 4
    e_d = (y_d % 2) * 8 + x_d * 2 + ((c + owner) % 2)[None, :, None]
    row = jnp.arange(2 * cap, dtype=jnp.int32)
    slots = e_d[:, :, :, None] * cap + row % cap
    hits = slots[:, :, :, :, None, None] == placed
    weight = jnp.sum(jnp.where(hits, route_weights, 0.0), axis=(4, 5))
    slot = jnp.where(row < cap, 1.0, weight)[:, :, :, :, None]
    chosen = jnp.any(hits, axis=5)
    kind = (row < cap)[:, None]
    sel = jnp.concatenate([chosen & kind, chosen & ~kind], axis=4).astype(BF)

    dense_cat = jnp.concatenate([dense_gate, dense_up, dense_down.T], axis=1)
    input_grad, output, dense_grad, expert_grad = layer_call(
        sel, slot, tokens, cotangent, dense_cat, expert_gate[0].T, expert_up[0].T, expert_down[0]
    )
    return (
        output.reshape(count, width),
        input_grad.reshape(count, width),
        dense_grad[:, :hid],
        dense_grad[:, hid : 2 * hid],
        dense_grad[:, 2 * hid :].T,
        expert_grad[:hid].T[None],
        expert_grad[hid : 2 * hid].T[None],
        expert_grad[2 * hid :][None],
    )


def solution(mesh):
    in_specs = (
        P(("dp", "expert"), None),
        P(("dp", "expert"), None),
        P(("dp", "expert"), "tensor"),
        P(("dp", "expert"), "tensor"),
        P("tensor", ("dp", "expert")),
        P("expert", "dp", "tensor"),
        P("expert", "dp", "tensor"),
        P("expert", "tensor", "dp"),
        P(("dp", "expert"), None),
        P(("dp", "expert"), None),
    )
    out_specs = (
        P(("dp", "expert"), None),
        P(("dp", "expert"), None),
        P(("dp", "expert"), "tensor"),
        P(("dp", "expert"), "tensor"),
        P("tensor", ("dp", "expert")),
        P("expert", "dp", "tensor"),
        P("expert", "dp", "tensor"),
        P("expert", "tensor", "dp"),
    )
    return jax.shard_map(shards, mesh=mesh, in_specs=in_specs, out_specs=out_specs, check_vma=False)
```

```python
import functools

import jax
import jax.numpy as jnp
from jax import lax
from jax.experimental import pallas as pl
from jax.experimental.pallas import tpu as pltpu
from jax.sharding import PartitionSpec as P

MESH = pl.DeviceIdType.MESH
BF = jnp.bfloat16
F32 = jnp.float32
HBM = pl.BlockSpec(memory_space=pl.ANY)
VMEM = pl.BlockSpec(memory_space=pltpu.VMEM)
DMA = pltpu.SemaphoreType.DMA
ROWS_A = pl.ds(0, 48)
ROWS_B = pl.ds(48, 64)
ROWS_A0, ROWS_A1 = pl.ds(0, 16), pl.ds(16, 32)
ROWS_B0, ROWS_B1 = pl.ds(48, 32), pl.ds(80, 32)
LOW, HIGH = pl.ds(0, 2), pl.ds(2, 2)


def silu_pair(values):
    logistic = jax.nn.sigmoid(values)
    return (values * logistic, logistic * (1.0 + values * (1.0 - logistic)))


def product(left, right):
    return jnp.dot(left, right, preferred_element_type=F32)


def times_transposed(left, right):
    return lax.dot_general(left, right, (((1,), (1,)), ((), ())), preferred_element_type=F32)


def transposed_times(left, right):
    return lax.dot_general(left, right, (((0,), (0,)), ((), ())), preferred_element_type=F32)


def place():
    dp, e, z = lax.axis_index("dp"), lax.axis_index("expert"), lax.axis_index("tensor")
    return dp * 2 + e // 8, (e // 2) % 4, e % 2, z


def device(y, x, c, z):
    return (y // 2, (y % 2) * 8 + x * 2 + c, z)


def dispatch_dest(y, x, c, owner, j):
    return (y + j) % 4, (x + owner // 2 + 2 * (j % 2)) % 4, (c + owner) % 2


def dispatch_source(y, x, c, owner, j):
    return (y + 4 - j) % 4, (x + 8 - owner // 2 - 2 * (j % 2)) % 4, (c + owner) % 2


def remote(src, dst, send_sem, recv_sem, dev):
    return pltpu.make_async_remote_copy(
        src_ref=src, dst_ref=dst, send_sem=send_sem, recv_sem=recv_sem, device_id=dev, device_id_type=MESH
    )


def greet(devices, conditional=()):
    barrier = pltpu.get_barrier_semaphore()
    for dev in devices:
        pl.semaphore_signal(barrier, inc=1, device_id=dev, device_id_type=MESH)
    for cond, dev in conditional:
        @pl.when(cond)
        def _():
            pl.semaphore_signal(barrier, inc=1, device_id=dev, device_id_type=MESH)
    count = jnp.int32(len(devices))
    for cond, dev in conditional:
        count = count + jnp.where(cond, jnp.int32(1), jnp.int32(0))
    pl.semaphore_wait(barrier, count)


def add_into(dst, *others):
    total = dst[...].astype(F32)
    for other in others:
        total = total + other[...].astype(F32)
    dst[...] = total.astype(BF)


ORDER = (0, 3, -3, 4, -1, 1, -2, 2)
DIRECT = 3
HOME = (0, 3)


def layer_kernel(
    sel, slot, tokens, cots, w, gate, up, down,
    back, out, dgrad, ggrad, ugrad, lgrad,
    send, wt, recv, full, cr, mine, theirs, via, acts, spread, part, rr, ra, rb, rc, rd, ret, tot, rz,
    wt_s, dsp_s, dsp_r, ag_s, ag_r, loc, da_s, da_r, near_s, near_r, far_s, far_r,
    ring_s, ring_r, ret_s, ret_r, d_s, d_r, rs_s, rs_r, fin_s, fin_r,
):
    y, x, c, z = place()
    hid, half = gate.shape
    right, left = device(y, x, c, (z + 1) % 8), device(y, x, c, (z + 7) % 8)
    xp, xm, yp, ym = (x + 1) % 4, (x + 3) % 4, (y + 1) % 4, (y + 3) % 4
    east, west = device(y, xp, c, z), device(y, xm, c, z)
    above, below = device(yp, x, c, z), device(ym, x, c, z)
    other = device(y, x, 1 - c, z)

    def block(r):
        return (z + 8 + ORDER[r]) % 8

    def dest(r, j):
        return device(*dispatch_dest(y, x, c, block(r), j), z)

    def source(r, j):
        return device(*dispatch_source(y, x, c, block(r), j), z)

    greet(
        [source(r, j) for r in range(DIRECT) for j in (1, 2, 3)]
        + [dest(r, j) for r in HOME for j in (1, 2, 3)]
        + [east, west, above, below, other, left, right],
        [(block(r) != 0, source(r, 0)) for r in range(DIRECT)] + [(block(r) != 0, dest(r, 0)) for r in HOME],
    )
    weights = [
        pltpu.make_async_copy(ref, wt.at[pl.ds(i * hid, hid)], wt_s.at[i]) for i, ref in enumerate((gate, up, down))
    ]
    for copy in weights:
        copy.start()


    def build(r):
        for h in (0, 1):
            cols = slice(h * half, (h + 1) * half)
            chosen = sel[h, r].reshape(96, 256)
            value = product(chosen[:, :128], tokens[:, cols]) + product(chosen[:, 128:], cots[:, cols])
            send[h, r] = (value * slot[h, r].reshape(96, 1)).astype(BF).reshape(2, 48, half)

    def straight(j, r, src, dst, send_sem, recv_sem, dev, action):
        copy = remote(src, dst, send_sem, recv_sem, dev)
        if j:
            getattr(copy, action)()
            return

        @pl.when(block(r) == 0)
        def _():
            if action != "wait_send":
                stay = pltpu.make_async_copy(src, dst, recv_sem)
                stay.start() if action == "start" else stay.wait()

        @pl.when(block(r) != 0)
        def _():
            getattr(copy, action)()

    def disp(r, j, action):
        y_d = (y + j) % 4
        straight(
            j, r, send.at[y_d // 2, r, y_d % 2], recv.at[block(r), y], dsp_s.at[r, j], dsp_r.at[r, j], dest(r, j), action
        )

    def carried(direction, t):
        return range(4) if t < 3 else ((0, 1), (2, 3))[direction]

    def carry_step(t):
        for j in range(4):
            for direction in (0, 1):
                carry(direction, t - 1, j).wait_recv()
                if j in carried(direction, t):
                    carry(direction, t, j).start()

    def carry(direction, t, j):
        ahead = t if t < 3 else 4
        origin = (z + 9 - ahead) % 8 if direction == 0 else (z + ahead - 1) % 8
        k = (y + 4 - j) % 4
        return remote(
            recv.at[origin, k], recv.at[origin, k],
            ag_s.at[direction, t - 1, j], ag_r.at[direction, t - 1, j], (right, left)[direction],
        )

    build(0)
    for j in range(4):
        disp(0, j, "start")
    for r in range(1, DIRECT):
        build(r)
        for j in range(4):
            disp(r, j, "start")


    own = pltpu.make_async_copy(w, full.at[y, x, c], loc.at[0])
    own.start()

    def pass_on(stage, i, place_of, dev):
        return remote(place_of, place_of, da_s.at[stage, i], da_r.at[stage, i], dev)

    def first_send(i, rows, dev):
        return remote(w.at[rows], full.at[y, x, c, rows], da_s.at[0, i], da_r.at[0, i], dev)

    ga = [
        first_send(0, ROWS_A, east),
        first_send(1, ROWS_A, west),
        first_send(2, ROWS_B, above),
        first_send(3, ROWS_B, below),
    ]
    gb = [
        pass_on(1, 0, full.at[y, xm, c, ROWS_A0], east),
        pass_on(1, 1, full.at[y, xp, c, ROWS_A1], west),
        pass_on(1, 2, full.at[ym, x, c, ROWS_B0], above),
        pass_on(1, 3, full.at[yp, x, c, ROWS_B1], below),
    ]
    gc = [
        pass_on(2, 0, full.at[y, :, c, ROWS_A], above),
        pass_on(2, 1, full.at[y, :, c, ROWS_A], below),
        pass_on(2, 2, full.at[:, x, c, ROWS_B], east),
        pass_on(2, 3, full.at[:, x, c, ROWS_B], west),
    ]
    gd = [
        pass_on(3, 0, full.at[ym, LOW, c, ROWS_A], above),
        pass_on(3, 1, full.at[yp, HIGH, c, ROWS_A], below),
        pass_on(3, 2, full.at[LOW, xm, c, ROWS_B], east),
        pass_on(3, 3, full.at[HIGH, xp, c, ROWS_B], west),
    ]
    ge = [pass_on(4, i, full.at[i, :, c], other) for i in range(4)]

    def after(earlier, later):
        for copy in earlier:
            copy.wait_recv()
        for copy in later:
            copy.start()


    def near(r, h):
        return remote(
            mine.at[block(r), h], via.at[block(r), h], near_s.at[r, h], near_r.at[r, h], (above, below)[h]
        )

    def far(r, h):
        return remote(
            via.at[block(r), h], theirs.at[block(r), h], far_s.at[r, h], far_r.at[r, h], (above, below)[h]
        )

    def pre_block(r):
        b = block(r)
        value = times_transposed(recv[b].reshape(192, half), wt[...]).reshape(4, 48, 3 * hid)
        lane = lax.broadcasted_iota(jnp.int32, (4, 24, 3 * hid), 2)
        value = jnp.where(lane < 2 * hid, value[:, :24], value[:, 24:])
        mine[b] = value.reshape(2, 48, 3 * hid).astype(BF)
        for h in (0, 1):
            near(r, h).start()

    def relay(r):
        for h in (0, 1):
            near(r, h).wait_recv()
            far(r, h).start()


    def results_block(r):
        b = block(r)
        for h in (0, 1):
            far(r, h).wait_recv()
        pre = (mine[b].astype(F32) + theirs[b].astype(F32)).reshape(4, 24, 3 * hid)
        pre_up, grad_act = pre[:, :, hid : 2 * hid], pre[:, :, 2 * hid :]
        active, slope = silu_pair(pre[:, :, :hid])
        zeros = jnp.zeros((4, 24, hid), F32)
        first = jnp.concatenate([grad_act * pre_up * slope, grad_act * active, zeros], axis=2)
        second = jnp.concatenate([zeros, zeros, active * pre_up], axis=2)
        acts[b] = jnp.concatenate([first, second], axis=1).astype(BF)
        part[b] = product(acts[b].reshape(192, 3 * hid), wt[...]).astype(BF).reshape(4, 48, half)


    def dense_forward():
        both = jnp.concatenate([tokens[...], cots[...]], axis=0)
        pre = product(both, full[...].reshape(both.shape[1], 3 * hid))
        active, slope = silu_pair(pre[:128, :hid])
        pre_up = pre[:128, hid : 2 * hid]
        grad_act = pre[128:, 2 * hid :]
        zeros = jnp.zeros((128, hid), F32)
        spread[0:128, :] = jnp.concatenate(
            [grad_act * pre_up * slope, grad_act * active, zeros], axis=1
        ).astype(BF)
        spread[128:256, :] = jnp.concatenate([zeros, zeros, active * pre_up], axis=1).astype(BF)

        @pl.loop(0, 4)
        def _(i):
            rows = full[i].reshape(896, 3 * hid)
            value = times_transposed(spread[...], rows).astype(BF)
            tot[:, :, :, pl.ds(pl.multiple_of(i * 896, 128), 896)] = value.reshape(2, 8, 16, 896)

    def dense_weights():
        @pl.loop(0, 4)
        def _(i):
            cols = pl.ds(pl.multiple_of(i * 896, 128), 896)
            value = transposed_times(tokens[:, cols], spread[0:128, :])
            value = value + transposed_times(cots[:, cols], spread[128:256, :])
            full[i] = value.astype(BF).reshape(4, 2, 112, 3 * hid)


    def target(direction, v):
        return (z + 4 - v) % 8 if direction == 0 else (z + 4 + v) % 8

    def hop(direction, v, k):
        src = part.at[target(direction, 1), k] if v == 1 else rr.at[direction, v - 2, k]
        return remote(
            src, rr.at[direction, v - 1, k],
            ring_s.at[direction, v - 1, k], ring_r.at[direction, v - 1, k], (right, left)[direction],
        )

    def ring_step(v):
        for k in range(4):
            for direction in (0, 1):
                hop(direction, v - 1, k).wait_recv()
                add_into(rr.at[direction, v - 2, k], part.at[target(direction, v), k])
                hop(direction, v, k).start()

    def home(r, j, action):
        k = (y + 4 - j) % 4
        src = rr.at[0, 2, k] if r == 0 else part.at[block(r), k]
        straight(j, r, src, ret.at[r // 3, y], ret_s.at[r // 3, j], ret_r.at[r // 3, j], source(r, j), action)


    def partial(stage, i, src, dst, dev):
        return remote(src, dst, d_s.at[stage, i], d_r.at[stage, i], dev)

    yo, xo = (y + 2) % 4, (x + 2) % 4
    s_one = [partial(0, i, full.at[i, :, 1 - c], cr.at[i], other) for i in range(4)]
    s_two = [
        partial(1, 0, cr.at[yo, LOW, ROWS_A], ra.at[0, LOW], above),
        partial(1, 1, cr.at[yo, HIGH, ROWS_A], ra.at[0, HIGH], below),
        partial(1, 2, cr.at[LOW, xo, ROWS_B], rb.at[0, LOW], east),
        partial(1, 3, cr.at[HIGH, xo, ROWS_B], rb.at[0, HIGH], west),
    ]
    s_three = [
        partial(2, 0, cr.at[yp, :, ROWS_A], ra.at[1], above),
        partial(2, 1, cr.at[ym, :, ROWS_A], ra.at[2], below),
        partial(2, 2, cr.at[:, xp, ROWS_B], rb.at[1], east),
        partial(2, 3, cr.at[:, xm, ROWS_B], rb.at[2], west),
    ]
    s_four = [
        partial(3, 0, cr.at[y, xo, ROWS_A0], rc.at[0, ROWS_A0], east),
        partial(3, 1, cr.at[y, xo, ROWS_A1], rc.at[0, ROWS_A1], west),
        partial(3, 2, cr.at[yo, x, ROWS_B0], rd.at[0, pl.ds(0, 32)], above),
        partial(3, 3, cr.at[yo, x, ROWS_B1], rd.at[0, pl.ds(32, 32)], below),
    ]
    s_five = [
        partial(4, 0, cr.at[y, xp, ROWS_A], rc.at[1], east),
        partial(4, 1, cr.at[y, xm, ROWS_A], rc.at[2], west),
        partial(4, 2, cr.at[yp, x, ROWS_B], rd.at[1], above),
        partial(4, 3, cr.at[ym, x, ROWS_B], rd.at[2], below),
    ]

    def scatter_two():
        for copy in s_one:
            copy.wait_recv()

        @pl.loop(0, 16)
        def _(i):
            add_into(cr.at[i // 4, i % 4], full.at[i // 4, i % 4, c])

        for copy in s_two:
            copy.start()

    def scatter_three():
        for copy in s_two:
            copy.wait_recv()

        @pl.loop(0, 2)
        def _(i):
            add_into(cr.at[yp, i, ROWS_A], ra.at[0, i])
            add_into(cr.at[ym, i + 2, ROWS_A], ra.at[0, i + 2])
            add_into(cr.at[i, xp, ROWS_B], rb.at[0, i])
            add_into(cr.at[i + 2, xm, ROWS_B], rb.at[0, i + 2])

        for copy in s_three:
            copy.start()

    def scatter_four():
        for copy in s_three:
            copy.wait_recv()

        @pl.loop(0, 4)
        def _(i):
            add_into(cr.at[y, i, ROWS_A], ra.at[1, i], ra.at[2, i])
            add_into(cr.at[i, x, ROWS_B], rb.at[1, i], rb.at[2, i])

        for copy in s_four:
            copy.start()

    def scatter_five():
        for copy in s_four:
            copy.wait_recv()
        add_into(cr.at[y, xp, ROWS_A0], rc.at[0, ROWS_A0])
        add_into(cr.at[y, xm, ROWS_A1], rc.at[0, ROWS_A1])
        add_into(cr.at[yp, x, ROWS_B0], rd.at[0, pl.ds(0, 32)])
        add_into(cr.at[ym, x, ROWS_B1], rd.at[0, pl.ds(32, 32)])
        for copy in s_five:
            copy.start()

    def scatter_end():
        for copy in s_five:
            copy.wait_recv()
        add_into(cr.at[y, x, ROWS_A], rc.at[1], rc.at[2])
        add_into(cr.at[y, x, ROWS_B], rd.at[1], rd.at[2])
        dgrad[...] = cr[y, x]


    def expert_weights(i):
        first, last = 256 * i, min(256 * (i + 1), 3 * hid)
        rows = acts[:, :, :, first:last].reshape(1536, last - first)
        value = transposed_times(rows, recv[...].reshape(1536, half)).astype(BF)
        for q, ref in enumerate((ggrad, ugrad, lgrad)):
            low, high = max(first, q * hid), min(last, (q + 1) * hid)
            if low < high:
                ref[low - q * hid : high - q * hid, :] = value[low - first : high - first]


    outs = (back, out)

    def final_target(direction, u):
        return (z + 5 - u) % 8 if direction == 0 else (z + 3 + u) % 8

    def final_hop(direction, u, q):
        fresh = u == 1 or (u == 2 and q != direction)
        src = tot.at[q, final_target(direction, u)] if fresh else rz.at[direction, u - 2, q]
        return remote(
            src, rz.at[direction, u - 1, q],
            rs_s.at[direction, u - 1, q], rs_r.at[direction, u - 1, q], (right, left)[direction],
        )

    def final_step(u):
        for q in (0, 1):
            for direction in (0, 1):
                if u == 2 and q != direction:
                    continue
                final_hop(direction, u - 1, q).wait_recv()
                add_into(rz.at[direction, u - 2, q], tot.at[q, final_target(direction, u)])
                final_hop(direction, u, q).start()

    def share(direction, t, q):
        origin = (z + 9 - t) % 8 if direction == 0 else (z + t - 1) % 8
        return remote(
            outs[q].at[origin], outs[q].at[origin],
            fin_s.at[direction, t - 1, q], fin_r.at[direction, t - 1, q], (right, left)[direction],
        )


    for j in range(4):
        disp(0, j, "wait_recv")
        carry(0, 1, j).start()
        carry(1, 1, j).start()
    for copy in ga:
        copy.start()
    for copy in weights:
        copy.wait()
    pre_block(0)
    carry_step(2)
    after(ga, gb)
    for r in range(1, DIRECT):
        for j in range(4):
            disp(r, j, "wait_recv")
        pre_block(r)
    relay(0)
    pre_block(4)
    pre_block(5)
    relay(1)
    relay(2)
    carry_step(3)
    for r in (1, 2):
        results_block(r)
        for k in range(4):
            hop(r - 1, 1, k).start()
    pre_block(6)
    pre_block(7)
    relay(4)
    relay(5)
    relay(6)
    relay(7)
    for direction in (0, 1):
        for j in carried(direction, 3):
            carry(direction, 3, j).wait_recv()
    pre_block(3)
    own.wait()
    after(gb, gc)
    results_block(6)
    results_block(7)
    ring_step(2)
    relay(3)
    results_block(4)
    results_block(5)
    results_block(3)
    for j in range(4):
        home(3, j, "start")
    ring_step(3)
    after(gc, gd)
    results_block(0)
    expert_weights(0)
    expert_weights(1)
    after(gd, ge)
    for k in range(4):
        hop(0, 3, k).wait_recv()
        hop(1, 3, k).wait_recv()
        add_into(rr.at[0, 2, k], rr.at[1, 2, k], part.at[z, k])
    for j in range(4):
        home(0, j, "start")
    after(ge, ())
    dense_forward()
    for copy in ga + gb + gc + gd + ge:
        copy.wait_send()
    dense_weights()
    for copy in s_one:
        copy.start()
    for r in HOME:
        for j in range(4):
            home(r, j, "wait_recv")
    for h in (0, 1):
        cols = slice(h * half, (h + 1) * half)
        value = jnp.zeros((256, half), F32)
        for i, r in enumerate(HOME):
            rows = ret[i, 2 * h : 2 * h + 2].reshape(96, half).astype(F32) * slot[h, r].reshape(96, 1)
            value = value + transposed_times(sel[h, r].reshape(96, 256), rows.astype(BF))
        value = value.reshape(2, 8, 16, half)
        tot[:, :, :, cols] = (tot[:, :, :, cols].astype(F32) + value).astype(BF)
    for direction in (0, 1):
        final_hop(direction, 1, direction).start()
    for direction in (0, 1):
        final_hop(direction, 2, 1 - direction).start()
    expert_weights(2)
    scatter_two()
    final_step(2)
    expert_weights(3)
    scatter_three()
    final_step(3)
    scatter_four()
    final_step(4)
    scatter_five()
    mine_rows = pl.ds(pl.multiple_of(z * 16, 16), 16)
    for q in (0, 1):
        final_hop(0, 4, q).wait_recv()
        final_hop(1, 4, q).wait_recv()
        total = rz[0, 3, q].astype(F32) + rz[1, 3, q].astype(F32) + tot[q, z].astype(F32)
        total = total + (cots, tokens)[q][mine_rows, :].astype(F32)
        outs[q][z] = total.astype(BF)
        for direction in (0, 1):
            share(direction, 1, q).start()
    for t in (2, 3, 4):
        for q in (0, 1):
            for direction in (0, 1):
                share(direction, t - 1, q).wait_recv()
                if t < 4 or q == direction:
                    share(direction, t, q).start()
    for direction in (0, 1):
        share(direction, 4, direction).wait_recv()
    scatter_end()


    for r in range(DIRECT):
        for j in range(4):
            disp(r, j, "wait_send")
    for r in HOME:
        for j in range(4):
            home(r, j, "wait_send")
    for r in range(8):
        for h in (0, 1):
            near(r, h).wait_send()
            far(r, h).wait_send()
    for direction in (0, 1):
        for k in range(4):
            for t in (1, 2, 3):
                if k in carried(direction, t):
                    carry(direction, t, k).wait_send()
            for v in (1, 2, 3):
                hop(direction, v, k).wait_send()
        for u in (1, 2, 3, 4):
            for q in (0, 1):
                if u > 1 or q == direction:
                    final_hop(direction, u, q).wait_send()
                if u < 4 or q == direction:
                    share(direction, u, q).wait_send()
    for copy in s_one + s_two + s_three + s_four + s_five:
        copy.wait_send()


def layer_call(sel, slot, tokens, cots, w, gate, up, down):
    hid, half = gate.shape
    lanes = w.shape[1]
    count, width = tokens.shape
    shape = jax.ShapeDtypeStruct
    swap = pltpu.VMEM((8, 2, 48, lanes), BF)
    rows = pltpu.VMEM((8, 4, 48, half), BF)
    return pl.pallas_call(
        layer_kernel,
        out_shape=(
            shape((8, 16, width), BF),
            shape((8, 16, width), BF),
            shape((112, lanes), BF),
            shape((hid, half), BF),
            shape((hid, half), BF),
            shape((hid, half), BF),
        ),
        in_specs=[VMEM] * 4 + [HBM] * 4,
        out_specs=(VMEM,) * 6,
        scratch_shapes=[
            pltpu.VMEM((2, DIRECT, 2, 48, half), BF),
            pltpu.VMEM((lanes, half), BF),
            rows,
            pltpu.VMEM((4, 4, 2, 112, lanes), BF),
            pltpu.VMEM((4, 4, 112, lanes), BF),
            swap, swap, swap,
            pltpu.VMEM((8, 4, 48, lanes), BF),
            pltpu.VMEM((2 * count, lanes), BF),
            rows,
            pltpu.VMEM((2, 3, 4, 48, half), BF),
            pltpu.VMEM((3, 4, 48, lanes), BF),
            pltpu.VMEM((3, 4, 64, lanes), BF),
            pltpu.VMEM((3, 48, lanes), BF),
            pltpu.VMEM((3, 64, lanes), BF),
            pltpu.VMEM((len(HOME), 4, 48, half), BF),
            pltpu.VMEM((2, 8, 16, width), BF),
            pltpu.VMEM((2, 4, 2, 16, width), BF),
            DMA((3,)), DMA((DIRECT, 4)), DMA((DIRECT, 4)), DMA((2, 3, 4)), DMA((2, 3, 4)), DMA((1,)),
            DMA((5, 4)), DMA((5, 4)),
            DMA((8, 2)), DMA((8, 2)), DMA((8, 2)), DMA((8, 2)),
            DMA((2, 3, 4)), DMA((2, 3, 4)), DMA((len(HOME), 4)), DMA((len(HOME), 4)), DMA((5, 4)), DMA((5, 4)),
            DMA((2, 4, 2)), DMA((2, 4, 2)), DMA((2, 4, 2)), DMA((2, 4, 2)),
        ],
        compiler_params=pltpu.CompilerParams(
            collective_id=0, has_side_effects=True, vmem_limit_bytes=63 * 1024 * 1024
        ),
    )(sel, slot, tokens, cots, w, gate, up, down)


def shards(
    tokens,
    cotangent,
    dense_gate,
    dense_up,
    dense_down,
    expert_gate,
    expert_up,
    expert_down,
    expert_ids,
    route_weights,
):
    count, width = tokens.shape
    hid = dense_gate.shape[1]
    experts, cap = 16, 24
    y, x, c, z = place()

    flat_ids = expert_ids.reshape(-1)
    onehot = (flat_ids[:, None] == jnp.arange(experts, dtype=jnp.int32)[None, :]).astype(jnp.int32)
    earlier = jnp.cumsum(onehot, axis=0) - onehot
    placed = (flat_ids * cap + jnp.sum(earlier * onehot, axis=1)).reshape(count, 2)

    owner = (z + 8 + jnp.array(ORDER[:4], jnp.int32)) % 8
    y_d = jnp.arange(4, dtype=jnp.int32).reshape(2, 1, 2)
    x_d = (x + owner[None, :, None] // 2 + 2 * ((y_d + y) % 2)) % 4
    e_d = (y_d % 2) * 8 + x_d * 2 + ((c + owner) % 2)[None, :, None]
    row = jnp.arange(2 * cap, dtype=jnp.int32)
    slots = e_d[:, :, :, None] * cap + row % cap
    hits = slots[:, :, :, :, None, None] == placed
    weight = jnp.sum(jnp.where(hits, route_weights, 0.0), axis=(4, 5))
    slot = jnp.where(row < cap, 1.0, weight)[:, :, :, :, None]
    chosen = jnp.any(hits, axis=5)
    kind = (row < cap)[:, None]
    sel = jnp.concatenate([chosen & kind, chosen & ~kind], axis=4).astype(BF)

    dense_cat = jnp.concatenate([dense_gate, dense_up, dense_down.T], axis=1)
    input_grad, output, dense_grad, gate_grad, up_grad, down_grad = layer_call(
        sel, slot, tokens, cotangent, dense_cat, expert_gate[0].T, expert_up[0].T, expert_down[0]
    )
    return (
        output.reshape(count, width),
        input_grad.reshape(count, width),
        dense_grad[:, :hid],
        dense_grad[:, hid : 2 * hid],
        dense_grad[:, 2 * hid :].T,
        gate_grad.T[None],
        up_grad.T[None],
        down_grad[None],
    )


def solution(mesh):
    in_specs = (
        P(("dp", "expert"), None),
        P(("dp", "expert"), None),
        P(("dp", "expert"), "tensor"),
        P(("dp", "expert"), "tensor"),
        P("tensor", ("dp", "expert")),
        P("expert", "dp", "tensor"),
        P("expert", "dp", "tensor"),
        P("expert", "tensor", "dp"),
        P(("dp", "expert"), None),
        P(("dp", "expert"), None),
    )
    out_specs = (
        P(("dp", "expert"), None),
        P(("dp", "expert"), None),
        P(("dp", "expert"), "tensor"),
        P(("dp", "expert"), "tensor"),
        P("tensor", ("dp", "expert")),
        P("expert", "dp", "tensor"),
        P("expert", "dp", "tensor"),
        P("expert", "tensor", "dp"),
    )
    return jax.shard_map(shards, mesh=mesh, in_specs=in_specs, out_specs=out_specs, check_vma=False)
```

```python
import functools

import jax
import jax.numpy as jnp
from jax import lax
from jax.experimental import pallas as pl
from jax.experimental.pallas import tpu as pltpu
from jax.sharding import PartitionSpec as P

MESH = pl.DeviceIdType.MESH
BF = jnp.bfloat16
F32 = jnp.float32
HBM = pl.BlockSpec(memory_space=pl.ANY)
VMEM = pl.BlockSpec(memory_space=pltpu.VMEM)
DMA = pltpu.SemaphoreType.DMA
ROWS_A = pl.ds(0, 48)
ROWS_B = pl.ds(48, 64)
ROWS_A0, ROWS_A1 = pl.ds(0, 16), pl.ds(16, 32)
ROWS_B0, ROWS_B1 = pl.ds(48, 32), pl.ds(80, 32)
LOW, HIGH = pl.ds(0, 2), pl.ds(2, 2)


def silu_pair(values):
    logistic = jax.nn.sigmoid(values)
    return (values * logistic, logistic * (1.0 + values * (1.0 - logistic)))


def product(left, right):
    return jnp.dot(left, right, preferred_element_type=F32)


def times_transposed(left, right):
    return lax.dot_general(left, right, (((1,), (1,)), ((), ())), preferred_element_type=F32)


def transposed_times(left, right):
    return lax.dot_general(left, right, (((0,), (0,)), ((), ())), preferred_element_type=F32)


def place():
    dp, e, z = lax.axis_index("dp"), lax.axis_index("expert"), lax.axis_index("tensor")
    return dp * 2 + e // 8, (e // 2) % 4, e % 2, z


def device(y, x, c, z):
    return (y // 2, (y % 2) * 8 + x * 2 + c, z)


def dispatch_dest(y, x, c, owner, j):
    return (y + j) % 4, (x + owner // 2 + 2 * (j % 2)) % 4, (c + owner) % 2


def dispatch_source(y, x, c, owner, j):
    return (y + 4 - j) % 4, (x + 8 - owner // 2 - 2 * (j % 2)) % 4, (c + owner) % 2


def remote(src, dst, send_sem, recv_sem, dev):
    return pltpu.make_async_remote_copy(
        src_ref=src, dst_ref=dst, send_sem=send_sem, recv_sem=recv_sem, device_id=dev, device_id_type=MESH
    )


def greet(devices, conditional=()):
    barrier = pltpu.get_barrier_semaphore()
    for dev in devices:
        pl.semaphore_signal(barrier, inc=1, device_id=dev, device_id_type=MESH)
    for cond, dev in conditional:
        @pl.when(cond)
        def _():
            pl.semaphore_signal(barrier, inc=1, device_id=dev, device_id_type=MESH)
    count = jnp.int32(len(devices))
    for cond, dev in conditional:
        count = count + jnp.where(cond, jnp.int32(1), jnp.int32(0))
    pl.semaphore_wait(barrier, count)


def add_into(dst, *others):
    total = dst[...].astype(F32)
    for other in others:
        total = total + other[...].astype(F32)
    dst[...] = total.astype(BF)


ORDER = (0, 3, -3, 4, -1, 1, -2, 2)
DIRECT = 3
HOME = (0, 3)


def layer_kernel(
    sel, slot, tokens, cots, w, gate, up, down,
    back, out, dgrad, ggrad, ugrad, lgrad,
    send, wt, recv, full, cr, mine, theirs, via, acts, spread, part, rr, ra, rb, rc, rd, ret, tot, rz,
    wt_s, dsp_s, dsp_r, ag_s, ag_r, loc, da_s, da_r, near_s, near_r, far_s, far_r,
    ring_s, ring_r, ret_s, ret_r, d_s, d_r, rs_s, rs_r, fin_s, fin_r,
):
    y, x, c, z = place()
    hid, half = gate.shape
    right, left = device(y, x, c, (z + 1) % 8), device(y, x, c, (z + 7) % 8)
    xp, xm, yp, ym = (x + 1) % 4, (x + 3) % 4, (y + 1) % 4, (y + 3) % 4
    east, west = device(y, xp, c, z), device(y, xm, c, z)
    above, below = device(yp, x, c, z), device(ym, x, c, z)
    other = device(y, x, 1 - c, z)

    def block(r):
        return (z + 8 + ORDER[r]) % 8

    def dest(r, j):
        return device(*dispatch_dest(y, x, c, block(r), j), z)

    def source(r, j):
        return device(*dispatch_source(y, x, c, block(r), j), z)

    greet(
        [source(r, j) for r in range(DIRECT) for j in (1, 2, 3)]
        + [dest(r, j) for r in HOME for j in (1, 2, 3)]
        + [east, west, above, below, other, left, right],
        [(block(r) != 0, source(r, 0)) for r in range(DIRECT)] + [(block(r) != 0, dest(r, 0)) for r in HOME],
    )
    weights = [
        pltpu.make_async_copy(ref, wt.at[pl.ds(i * hid, hid)], wt_s.at[i]) for i, ref in enumerate((gate, up, down))
    ]
    for copy in weights:
        copy.start()


    def build(r):
        for h in (0, 1):
            cols = slice(h * half, (h + 1) * half)
            chosen = sel[h, r].reshape(96, 256)
            value = product(chosen[:, :128], tokens[:, cols]) + product(chosen[:, 128:], cots[:, cols])
            send[h, r] = (value * slot[h, r].reshape(96, 1)).astype(BF).reshape(2, 48, half)

    def straight(j, r, src, dst, send_sem, recv_sem, dev, action):
        copy = remote(src, dst, send_sem, recv_sem, dev)
        if j:
            getattr(copy, action)()
            return

        @pl.when(block(r) == 0)
        def _():
            if action != "wait_send":
                stay = pltpu.make_async_copy(src, dst, recv_sem)
                stay.start() if action == "start" else stay.wait()

        @pl.when(block(r) != 0)
        def _():
            getattr(copy, action)()

    def disp(r, j, action):
        y_d = (y + j) % 4
        straight(
            j, r, send.at[y_d // 2, r, y_d % 2], recv.at[block(r), y], dsp_s.at[r, j], dsp_r.at[r, j], dest(r, j), action
        )

    def carried(direction, t):
        return range(4) if t < 3 else ((0, 1), (2, 3))[direction]

    def carry_step(t):
        for j in range(4):
            for direction in (0, 1):
                carry(direction, t - 1, j).wait_recv()
                if j in carried(direction, t):
                    carry(direction, t, j).start()

    def carry(direction, t, j):
        ahead = t if t < 3 else 4
        origin = (z + 9 - ahead) % 8 if direction == 0 else (z + ahead - 1) % 8
        k = (y + 4 - j) % 4
        return remote(
            recv.at[origin, k], recv.at[origin, k],
            ag_s.at[direction, t - 1, j], ag_r.at[direction, t - 1, j], (right, left)[direction],
        )

    build(0)
    for j in range(4):
        disp(0, j, "start")
    for r in range(1, DIRECT):
        build(r)
        for j in range(4):
            disp(r, j, "start")


    own = pltpu.make_async_copy(w, full.at[y, x, c], loc.at[0])
    own.start()

    def pass_on(stage, i, place_of, dev):
        return remote(place_of, place_of, da_s.at[stage, i], da_r.at[stage, i], dev)

    def first_send(i, rows, dev):
        return remote(w.at[rows], full.at[y, x, c, rows], da_s.at[0, i], da_r.at[0, i], dev)

    ga = [
        first_send(0, ROWS_A, east),
        first_send(1, ROWS_A, west),
        first_send(2, ROWS_B, above),
        first_send(3, ROWS_B, below),
    ]
    gb = [
        pass_on(1, 0, full.at[y, xm, c, ROWS_A0], east),
        pass_on(1, 1, full.at[y, xp, c, ROWS_A1], west),
        pass_on(1, 2, full.at[ym, x, c, ROWS_B0], above),
        pass_on(1, 3, full.at[yp, x, c, ROWS_B1], below),
    ]
    gc = [
        pass_on(2, 0, full.at[y, :, c, ROWS_A], above),
        pass_on(2, 1, full.at[y, :, c, ROWS_A], below),
        pass_on(2, 2, full.at[:, x, c, ROWS_B], east),
        pass_on(2, 3, full.at[:, x, c, ROWS_B], west),
    ]
    gd = [
        pass_on(3, 0, full.at[ym, LOW, c, ROWS_A], above),
        pass_on(3, 1, full.at[yp, HIGH, c, ROWS_A], below),
        pass_on(3, 2, full.at[LOW, xm, c, ROWS_B], east),
        pass_on(3, 3, full.at[HIGH, xp, c, ROWS_B], west),
    ]
    ge = [pass_on(4, i, full.at[i, :, c], other) for i in range(4)]

    def after(earlier, later):
        for copy in earlier:
            copy.wait_recv()
        for copy in later:
            copy.start()


    def near(r, h):
        return remote(
            mine.at[block(r), h], via.at[block(r), h], near_s.at[r, h], near_r.at[r, h], (above, below)[h]
        )

    def far(r, h):
        return remote(
            via.at[block(r), h], theirs.at[block(r), h], far_s.at[r, h], far_r.at[r, h], (above, below)[h]
        )

    def pre_block(r):
        b = block(r)
        value = times_transposed(recv[b].reshape(192, half), wt[...]).reshape(4, 48, 3 * hid)
        lane = lax.broadcasted_iota(jnp.int32, (4, 24, 3 * hid), 2)
        value = jnp.where(lane < 2 * hid, value[:, :24], value[:, 24:])
        mine[b] = value.reshape(2, 48, 3 * hid).astype(BF)
        for h in (0, 1):
            near(r, h).start()

    def relay(r):
        for h in (0, 1):
            near(r, h).wait_recv()
            far(r, h).start()


    def results_block(r):
        b = block(r)
        for h in (0, 1):
            far(r, h).wait_recv()
        pre = (mine[b].astype(F32) + theirs[b].astype(F32)).reshape(4, 24, 3 * hid)
        pre_up, grad_act = pre[:, :, hid : 2 * hid], pre[:, :, 2 * hid :]
        active, slope = silu_pair(pre[:, :, :hid])
        zeros = jnp.zeros((4, 24, hid), F32)
        first = jnp.concatenate([grad_act * pre_up * slope, grad_act * active, zeros], axis=2)
        second = jnp.concatenate([zeros, zeros, active * pre_up], axis=2)
        acts[b] = jnp.concatenate([first, second], axis=1).astype(BF)
        part[b] = product(acts[b].reshape(192, 3 * hid), wt[...]).astype(BF).reshape(4, 48, half)


    def dense_forward():
        both = jnp.concatenate([tokens[...], cots[...]], axis=0)
        pre = product(both, full[...].reshape(both.shape[1], 3 * hid))
        active, slope = silu_pair(pre[:128, :hid])
        pre_up = pre[:128, hid : 2 * hid]
        grad_act = pre[128:, 2 * hid :]
        zeros = jnp.zeros((128, hid), F32)
        spread[0:128, :] = jnp.concatenate(
            [grad_act * pre_up * slope, grad_act * active, zeros], axis=1
        ).astype(BF)
        spread[128:256, :] = jnp.concatenate([zeros, zeros, active * pre_up], axis=1).astype(BF)

        @pl.loop(0, 4)
        def _(i):
            rows = full[i].reshape(896, 3 * hid)
            value = times_transposed(spread[...], rows).astype(BF)
            tot[:, :, :, pl.ds(pl.multiple_of(i * 896, 128), 896)] = value.reshape(2, 8, 16, 896)

    def dense_weights():
        @pl.loop(0, 4)
        def _(i):
            cols = pl.ds(pl.multiple_of(i * 896, 128), 896)
            value = transposed_times(tokens[:, cols], spread[0:128, :])
            value = value + transposed_times(cots[:, cols], spread[128:256, :])
            full[i] = value.astype(BF).reshape(4, 2, 112, 3 * hid)


    def target(direction, v):
        return (z + 4 - v) % 8 if direction == 0 else (z + 4 + v) % 8

    def hop(direction, v, k):
        src = part.at[target(direction, 1), k] if v == 1 else rr.at[direction, v - 2, k]
        return remote(
            src, rr.at[direction, v - 1, k],
            ring_s.at[direction, v - 1, k], ring_r.at[direction, v - 1, k], (right, left)[direction],
        )

    def ring_step(v):
        for k in range(4):
            for direction in (0, 1):
                hop(direction, v - 1, k).wait_recv()
                add_into(rr.at[direction, v - 2, k], part.at[target(direction, v), k])
                hop(direction, v, k).start()

    def home(r, j, action):
        k = (y + 4 - j) % 4
        src = rr.at[0, 2, k] if r == 0 else part.at[block(r), k]
        straight(j, r, src, ret.at[r // 3, y], ret_s.at[r // 3, j], ret_r.at[r // 3, j], source(r, j), action)


    def partial(stage, i, src, dst, dev):
        return remote(src, dst, d_s.at[stage, i], d_r.at[stage, i], dev)

    yo, xo = (y + 2) % 4, (x + 2) % 4
    s_one = [partial(0, i, full.at[i, :, 1 - c], cr.at[i], other) for i in range(4)]
    s_two = [
        partial(1, 0, cr.at[yo, LOW, ROWS_A], ra.at[0, LOW], above),
        partial(1, 1, cr.at[yo, HIGH, ROWS_A], ra.at[0, HIGH], below),
        partial(1, 2, cr.at[LOW, xo, ROWS_B], rb.at[0, LOW], east),
        partial(1, 3, cr.at[HIGH, xo, ROWS_B], rb.at[0, HIGH], west),
    ]
    s_three = [
        partial(2, 0, cr.at[yp, :, ROWS_A], ra.at[1], above),
        partial(2, 1, cr.at[ym, :, ROWS_A], ra.at[2], below),
        partial(2, 2, cr.at[:, xp, ROWS_B], rb.at[1], east),
        partial(2, 3, cr.at[:, xm, ROWS_B], rb.at[2], west),
    ]
    s_four = [
        partial(3, 0, cr.at[y, xo, ROWS_A0], rc.at[0, ROWS_A0], east),
        partial(3, 1, cr.at[y, xo, ROWS_A1], rc.at[0, ROWS_A1], west),
        partial(3, 2, cr.at[yo, x, ROWS_B0], rd.at[0, pl.ds(0, 32)], above),
        partial(3, 3, cr.at[yo, x, ROWS_B1], rd.at[0, pl.ds(32, 32)], below),
    ]
    s_five = [
        partial(4, 0, cr.at[y, xp, ROWS_A], rc.at[1], east),
        partial(4, 1, cr.at[y, xm, ROWS_A], rc.at[2], west),
        partial(4, 2, cr.at[yp, x, ROWS_B], rd.at[1], above),
        partial(4, 3, cr.at[ym, x, ROWS_B], rd.at[2], below),
    ]

    def scatter_two():
        for copy in s_one:
            copy.wait_recv()

        @pl.loop(0, 16)
        def _(i):
            add_into(cr.at[i // 4, i % 4], full.at[i // 4, i % 4, c])

        for copy in s_two:
            copy.start()

    def scatter_three():
        for copy in s_two:
            copy.wait_recv()

        @pl.loop(0, 2)
        def _(i):
            add_into(cr.at[yp, i, ROWS_A], ra.at[0, i])
            add_into(cr.at[ym, i + 2, ROWS_A], ra.at[0, i + 2])
            add_into(cr.at[i, xp, ROWS_B], rb.at[0, i])
            add_into(cr.at[i + 2, xm, ROWS_B], rb.at[0, i + 2])

        for copy in s_three:
            copy.start()

    def scatter_four():
        for copy in s_three:
            copy.wait_recv()

        @pl.loop(0, 4)
        def _(i):
            add_into(cr.at[y, i, ROWS_A], ra.at[1, i], ra.at[2, i])
            add_into(cr.at[i, x, ROWS_B], rb.at[1, i], rb.at[2, i])

        for copy in s_four:
            copy.start()

    def scatter_five():
        for copy in s_four:
            copy.wait_recv()
        add_into(cr.at[y, xp, ROWS_A0], rc.at[0, ROWS_A0])
        add_into(cr.at[y, xm, ROWS_A1], rc.at[0, ROWS_A1])
        add_into(cr.at[yp, x, ROWS_B0], rd.at[0, pl.ds(0, 32)])
        add_into(cr.at[ym, x, ROWS_B1], rd.at[0, pl.ds(32, 32)])
        for copy in s_five:
            copy.start()

    def scatter_end():
        for copy in s_five:
            copy.wait_recv()
        add_into(cr.at[y, x, ROWS_A], rc.at[1], rc.at[2])
        add_into(cr.at[y, x, ROWS_B], rd.at[1], rd.at[2])
        dgrad[...] = cr[y, x]


    def expert_weights(i):
        first, last = 256 * i, min(256 * (i + 1), 3 * hid)
        rows = acts[:, :, :, first:last].reshape(1536, last - first)
        value = transposed_times(rows, recv[...].reshape(1536, half)).astype(BF)
        for q, ref in enumerate((ggrad, ugrad, lgrad)):
            low, high = max(first, q * hid), min(last, (q + 1) * hid)
            if low < high:
                ref[low - q * hid : high - q * hid, :] = value[low - first : high - first]


    outs = (back, out)

    def final_target(direction, u):
        return (z + 5 - u) % 8 if direction == 0 else (z + 3 + u) % 8

    def final_hop(direction, u, q):
        fresh = u == 1 or (u == 2 and q != direction)
        src = tot.at[q, final_target(direction, u)] if fresh else rz.at[direction, u - 2, q]
        return remote(
            src, rz.at[direction, u - 1, q],
            rs_s.at[direction, u - 1, q], rs_r.at[direction, u - 1, q], (right, left)[direction],
        )

    def final_step(u):
        for q in (0, 1):
            for direction in (0, 1):
                if u == 2 and q != direction:
                    continue
                final_hop(direction, u - 1, q).wait_recv()
                add_into(rz.at[direction, u - 2, q], tot.at[q, final_target(direction, u)])
                final_hop(direction, u, q).start()

    def share(direction, t, q):
        origin = (z + 9 - t) % 8 if direction == 0 else (z + t - 1) % 8
        return remote(
            outs[q].at[origin], outs[q].at[origin],
            fin_s.at[direction, t - 1, q], fin_r.at[direction, t - 1, q], (right, left)[direction],
        )


    for j in range(4):
        disp(0, j, "wait_recv")
        carry(0, 1, j).start()
        carry(1, 1, j).start()
    for copy in ga:
        copy.start()
    for copy in weights:
        copy.wait()
    pre_block(0)
    carry_step(2)
    after(ga, gb)
    for r in range(1, DIRECT):
        for j in range(4):
            disp(r, j, "wait_recv")
        pre_block(r)
    relay(0)
    pre_block(4)
    pre_block(5)
    relay(1)
    relay(2)
    carry_step(3)
    for r in (1, 2):
        results_block(r)
        for k in range(4):
            hop(r - 1, 1, k).start()
    pre_block(6)
    pre_block(7)
    relay(4)
    relay(5)
    relay(6)
    relay(7)
    for direction in (0, 1):
        for j in carried(direction, 3):
            carry(direction, 3, j).wait_recv()
    pre_block(3)
    own.wait()
    after(gb, gc)
    results_block(6)
    results_block(7)
    ring_step(2)
    relay(3)
    results_block(4)
    results_block(5)
    results_block(3)
    for j in range(4):
        home(3, j, "start")
    ring_step(3)
    after(gc, gd)
    results_block(0)
    expert_weights(0)
    expert_weights(1)
    after(gd, ge)
    for k in range(4):
        hop(0, 3, k).wait_recv()
        hop(1, 3, k).wait_recv()
        add_into(rr.at[0, 2, k], rr.at[1, 2, k], part.at[z, k])
    for j in range(4):
        home(0, j, "start")
    after(ge, ())
    dense_forward()
    for copy in ga + gb + gc + gd + ge:
        copy.wait_send()
    dense_weights()
    for copy in s_one:
        copy.start()
    for r in HOME:
        for j in range(4):
            home(r, j, "wait_recv")
    for h in (0, 1):
        cols = slice(h * half, (h + 1) * half)
        value = jnp.zeros((256, half), F32)
        for i, r in enumerate(HOME):
            rows = ret[i, 2 * h : 2 * h + 2].reshape(96, half).astype(F32) * slot[h, r].reshape(96, 1)
            value = value + transposed_times(sel[h, r].reshape(96, 256), rows.astype(BF))
        value = value.reshape(2, 8, 16, half)
        tot[:, :, :, cols] = (tot[:, :, :, cols].astype(F32) + value).astype(BF)
    for direction in (0, 1):
        final_hop(direction, 1, direction).start()
    for direction in (0, 1):
        final_hop(direction, 2, 1 - direction).start()
    expert_weights(2)
    scatter_two()
    final_step(2)
    expert_weights(3)
    final_step(3)
    scatter_three()
    final_step(4)
    mine_rows = pl.ds(pl.multiple_of(z * 16, 16), 16)
    for q in (0, 1):
        final_hop(0, 4, q).wait_recv()
        final_hop(1, 4, q).wait_recv()
        total = rz[0, 3, q].astype(F32) + rz[1, 3, q].astype(F32) + tot[q, z].astype(F32)
        total = total + (cots, tokens)[q][mine_rows, :].astype(F32)
        outs[q][z] = total.astype(BF)
        for direction in (0, 1):
            share(direction, 1, q).start()
    scatter_four()
    for t in (2, 3, 4):
        for q in (0, 1):
            for direction in (0, 1):
                share(direction, t - 1, q).wait_recv()
                if t < 4 or q == direction:
                    share(direction, t, q).start()
        if t == 2:
            scatter_five()
    for direction in (0, 1):
        share(direction, 4, direction).wait_recv()
    scatter_end()


    for r in range(DIRECT):
        for j in range(4):
            disp(r, j, "wait_send")
    for r in HOME:
        for j in range(4):
            home(r, j, "wait_send")
    for r in range(8):
        for h in (0, 1):
            near(r, h).wait_send()
            far(r, h).wait_send()
    for direction in (0, 1):
        for k in range(4):
            for t in (1, 2, 3):
                if k in carried(direction, t):
                    carry(direction, t, k).wait_send()
            for v in (1, 2, 3):
                hop(direction, v, k).wait_send()
        for u in (1, 2, 3, 4):
            for q in (0, 1):
                if u > 1 or q == direction:
                    final_hop(direction, u, q).wait_send()
                if u < 4 or q == direction:
                    share(direction, u, q).wait_send()
    for copy in s_one + s_two + s_three + s_four + s_five:
        copy.wait_send()


def layer_call(sel, slot, tokens, cots, w, gate, up, down):
    hid, half = gate.shape
    lanes = w.shape[1]
    count, width = tokens.shape
    shape = jax.ShapeDtypeStruct
    swap = pltpu.VMEM((8, 2, 48, lanes), BF)
    rows = pltpu.VMEM((8, 4, 48, half), BF)
    return pl.pallas_call(
        layer_kernel,
        out_shape=(
            shape((8, 16, width), BF),
            shape((8, 16, width), BF),
            shape((112, lanes), BF),
            shape((hid, half), BF),
            shape((hid, half), BF),
            shape((hid, half), BF),
        ),
        in_specs=[VMEM] * 4 + [HBM] * 4,
        out_specs=(VMEM,) * 6,
        scratch_shapes=[
            pltpu.VMEM((2, DIRECT, 2, 48, half), BF),
            pltpu.VMEM((lanes, half), BF),
            rows,
            pltpu.VMEM((4, 4, 2, 112, lanes), BF),
            pltpu.VMEM((4, 4, 112, lanes), BF),
            swap, swap, swap,
            pltpu.VMEM((8, 4, 48, lanes), BF),
            pltpu.VMEM((2 * count, lanes), BF),
            rows,
            pltpu.VMEM((2, 3, 4, 48, half), BF),
            pltpu.VMEM((3, 4, 48, lanes), BF),
            pltpu.VMEM((3, 4, 64, lanes), BF),
            pltpu.VMEM((3, 48, lanes), BF),
            pltpu.VMEM((3, 64, lanes), BF),
            pltpu.VMEM((len(HOME), 4, 48, half), BF),
            pltpu.VMEM((2, 8, 16, width), BF),
            pltpu.VMEM((2, 4, 2, 16, width), BF),
            DMA((3,)), DMA((DIRECT, 4)), DMA((DIRECT, 4)), DMA((2, 3, 4)), DMA((2, 3, 4)), DMA((1,)),
            DMA((5, 4)), DMA((5, 4)),
            DMA((8, 2)), DMA((8, 2)), DMA((8, 2)), DMA((8, 2)),
            DMA((2, 3, 4)), DMA((2, 3, 4)), DMA((len(HOME), 4)), DMA((len(HOME), 4)), DMA((5, 4)), DMA((5, 4)),
            DMA((2, 4, 2)), DMA((2, 4, 2)), DMA((2, 4, 2)), DMA((2, 4, 2)),
        ],
        compiler_params=pltpu.CompilerParams(
            collective_id=0, has_side_effects=True, vmem_limit_bytes=63 * 1024 * 1024
        ),
    )(sel, slot, tokens, cots, w, gate, up, down)


def shards(
    tokens,
    cotangent,
    dense_gate,
    dense_up,
    dense_down,
    expert_gate,
    expert_up,
    expert_down,
    expert_ids,
    route_weights,
):
    count, width = tokens.shape
    hid = dense_gate.shape[1]
    experts, cap = 16, 24
    y, x, c, z = place()

    flat_ids = expert_ids.reshape(-1)
    onehot = (flat_ids[:, None] == jnp.arange(experts, dtype=jnp.int32)[None, :]).astype(jnp.int32)
    earlier = jnp.cumsum(onehot, axis=0) - onehot
    placed = (flat_ids * cap + jnp.sum(earlier * onehot, axis=1)).reshape(count, 2)

    owner = (z + 8 + jnp.array(ORDER[:4], jnp.int32)) % 8
    y_d = jnp.arange(4, dtype=jnp.int32).reshape(2, 1, 2)
    x_d = (x + owner[None, :, None] // 2 + 2 * ((y_d + y) % 2)) % 4
    e_d = (y_d % 2) * 8 + x_d * 2 + ((c + owner) % 2)[None, :, None]
    row = jnp.arange(2 * cap, dtype=jnp.int32)
    slots = e_d[:, :, :, None] * cap + row % cap
    hits = slots[:, :, :, :, None, None] == placed
    weight = jnp.sum(jnp.where(hits, route_weights, 0.0), axis=(4, 5))
    slot = jnp.where(row < cap, 1.0, weight)[:, :, :, :, None]
    chosen = jnp.any(hits, axis=5)
    kind = (row < cap)[:, None]
    sel = jnp.concatenate([chosen & kind, chosen & ~kind], axis=4).astype(BF)

    dense_cat = jnp.concatenate([dense_gate, dense_up, dense_down.T], axis=1)
    input_grad, output, dense_grad, gate_grad, up_grad, down_grad = layer_call(
        sel, slot, tokens, cotangent, dense_cat, expert_gate[0].T, expert_up[0].T, expert_down[0]
    )
    return (
        output.reshape(count, width),
        input_grad.reshape(count, width),
        dense_grad[:, :hid],
        dense_grad[:, hid : 2 * hid],
        dense_grad[:, 2 * hid :].T,
        gate_grad.T[None],
        up_grad.T[None],
        down_grad[None],
    )


def solution(mesh):
    in_specs = (
        P(("dp", "expert"), None),
        P(("dp", "expert"), None),
        P(("dp", "expert"), "tensor"),
        P(("dp", "expert"), "tensor"),
        P("tensor", ("dp", "expert")),
        P("expert", "dp", "tensor"),
        P("expert", "dp", "tensor"),
        P("expert", "tensor", "dp"),
        P(("dp", "expert"), None),
        P(("dp", "expert"), None),
    )
    out_specs = (
        P(("dp", "expert"), None),
        P(("dp", "expert"), None),
        P(("dp", "expert"), "tensor"),
        P(("dp", "expert"), "tensor"),
        P("tensor", ("dp", "expert")),
        P("expert", "dp", "tensor"),
        P("expert", "dp", "tensor"),
        P("expert", "tensor", "dp"),
    )
    return jax.shard_map(shards, mesh=mesh, in_specs=in_specs, out_specs=out_specs, check_vma=False)
```
